32 devices in a mesh: section: 2 (over x), tensor: 4 (over y, core), dp: 4 (over z).
Axes of the slice: x: 2, y: 2, z: 4, core: 2. Of those that a mesh axis runs over, the one named last changes fastest.
Arguments:
- boundary: bfloat16 [2, 2, 4, 1024, 1024], P('section', None, 'dp', 'tensor'), may hold values from -13 to 13
- segments: int32 [2, 4, 1024], P(None, 'dp'), may hold values from 0 to 4, as said below
- gains: float32 [2, 3, 1024], P('section'), may hold values from 0.5 to 1.5
- biases: float32 [2, 3, 1024], P('section'), may hold values from -1.75 to 1.75
- qkv_weight: bfloat16 [2, 1024, 3072], P('section', None, 'tensor'), may hold values from -0.1875 to 0.1875
- qv_bias: float32 [2, 2, 1024], P('section', None, 'tensor'), may hold values from -1.75 to 1.75
- out_weight: bfloat16 [2, 1024, 1024], P('section', 'tensor'), may hold values from -0.375 to 0.375
- out_bias: float32 [2, 1024], P('section'), may hold values from -1.75 to 1.75
- up_weight: bfloat16 [2, 1024, 4096], P('section', None, 'tensor'), may hold values from -0.1875 to 0.1875
- up_bias: float32 [2, 4096], P('section', 'tensor'), may hold values from -1.75 to 1.75
- down_weight: bfloat16 [2, 4096, 1024], P('section', 'tensor'), may hold values from -0.09375 to 0.09375
- down_bias: float32 [2, 1024], P('section'), may hold values from -1.75 to 1.75
Outputs:
- ends_out: float32 [2, 2, 4, 1024, 1024], P('section', None, 'dp', 'tensor')
- embed_stat: float32 [], replicated
- gain_grads: float32 [2, 3, 1024], P('section')
- bias_grads: float32 [2, 3, 1024], P('section')
- qkv_grad: float32 [2, 1024, 3072], P('section', None, 'tensor')
- qv_bias_grad: float32 [2, 2, 1024], P('section', None, 'tensor')
- out_grad: float32 [2, 1024, 1024], P('section', 'tensor')
- out_bias_grad: float32 [2, 1024], P('section')
- up_grad: float32 [2, 1024, 4096], P('section', None, 'tensor')
- up_bias_grad: float32 [2, 4096], P('section', 'tensor')
- down_grad: float32 [2, 4096, 1024], P('section', 'tensor')
- down_bias_grad: float32 [2, 1024], P('section')
The draws below stay inside these ranges and needn't reach their ends.
Inputs may be any that keep to these rules, and one draw needn't show every extreme that they name: `segments`: along each row the ids start at 0 and never fall; every row holds ids 0 to 4.
All inputs are finite; a program needn't handle non-finite values.
Results may differ from the reference program's by a relative error of at most 0.019.
Values may be sent and summed in bfloat16 or wider, within the bound.
No kernel may reach another device: no remote copies, remote signals or barrier semaphores. Data moves between devices by JAX's collectives and lax.ppermute only.
A program may use at most 256 MiB of HBM per device.

```python
import math
from functools import partial
import jax
import jax.numpy as jnp
from jax import lax

D = 1024
H = 16
HD = 64
FF = 4096
SEQ = 1024
MB = 2
ROWS = 4


def draw_boundary(key, part):
    key = jax.random.fold_in(key, 5)
    base_key, offset_key = jax.random.split(key)
    shape = (2, MB, ROWS, SEQ, D)
    row_place = jnp.arange(ROWS, dtype=jnp.float32).reshape(1, 1, ROWS, 1, 1) / ROWS
    token_place = jnp.arange(SEQ, dtype=jnp.float32).reshape(1, 1, 1, SEQ, 1) / SEQ
    base = jnp.clip(jax.random.normal(base_key, shape, jnp.float32), -6.0, 6.0)
    power = 0.5
    offset = jax.random.uniform(offset_key, (1, MB, ROWS, SEQ, 1), jnp.float32, 0.3, 0.8)
    chosen = (jnp.arange(2, dtype=jnp.int32).reshape(2, 1, 1, 1, 1) == 1).astype(jnp.float32)
    scale = 0.6 * jnp.exp(power * math.log(3.0) * (row_place + token_place))
    return ((base + chosen * offset) * scale).astype(jnp.bfloat16)


def draw_segments(key, part):
    key = jax.random.fold_in(key, 7)
    first_key, second_key, third_key, fourth_key = jax.random.split(key, 4)
    shape = (MB, ROWS, 1)
    opening = jax.random.randint(first_key, shape, 2, max(SEQ // 8, 3))
    early = jax.random.randint(second_key, shape, 1, opening)
    closing = jax.random.randint(third_key, shape, 7 * SEQ // 8, SEQ - 1)
    late = jax.random.randint(fourth_key, shape, closing + 1, SEQ)
    places = jnp.arange(SEQ, dtype=jnp.int32).reshape(1, 1, SEQ)
    ids = (places >= early).astype(jnp.int32) + (places >= opening).astype(jnp.int32)
    ids = ids + (places >= closing).astype(jnp.int32) + (places >= late).astype(jnp.int32)
    return ids


def steps_of(rng, extent, shards, low, top_value):
    level = 1.0
    for position, shards_of in shards:
        heights = jax.random.uniform(jax.random.fold_in(jax.random.fold_in(rng, 6), position), (shards_of,), jnp.float32, low / len(shards), top_value / len(shards))
        level = level * jnp.repeat(jnp.exp(heights), extent[position] // shards_of).reshape((-1,) + (1,) * (len(extent) - 1 - position))
    return level


def bell_draw(rng, dims, scale, bound, cuts=(), held_as=jnp.bfloat16):
    result = scale * jax.random.normal(rng, dims, jnp.float32)
    if cuts:
        result = result * steps_of(rng, dims, cuts, -0.22, 0.18)
    return jnp.clip(result, -bound, bound).astype(held_as)


def setup_inputs(seed: int = 0) -> dict:
    key_of = jax.random.split(jax.random.key(seed), 13)
    boundary = draw_boundary(jax.random.fold_in(key_of[12], 71), 0)
    segments = draw_segments(jax.random.fold_in(key_of[12], 71), 0)
    gains = jnp.clip(1.0 + 0.1 * jax.random.normal(key_of[2], (2, 3, D), jnp.float32), 0.5, 1.5)
    biases = bell_draw(key_of[3], (2, 3, D), 0.3, 1.75, ((0, 2),), jnp.float32)
    qkv_weight = bell_draw(key_of[4], (2, D, 3 * D), D ** -0.5, 0.1875, ((0, 2), (2, 4)))
    qv_bias = bell_draw(key_of[5], (2, 2, D), 0.3, 1.75, ((0, 2), (2, 4)), jnp.float32)
    out_weight = bell_draw(key_of[6], (2, D, D), (D // 4) ** -0.5, 0.375, ((0, 2), (1, 4)))
    out_bias = bell_draw(key_of[7], (2, D), 0.3, 1.75, ((0, 2),), jnp.float32)
    up_weight = bell_draw(key_of[8], (2, D, FF), D ** -0.5, 0.1875, ((0, 2), (2, 4)))
    up_bias = bell_draw(key_of[9], (2, FF), 0.3, 1.75, ((0, 2), (1, 4)), jnp.float32)
    down_weight = bell_draw(key_of[10], (2, FF, D), FF ** -0.5, 0.09375, ((0, 2), (1, 4)))
    down_bias = bell_draw(key_of[11], (2, D), 0.3, 1.75, ((0, 2),), jnp.float32)
    return {"boundary": boundary, "segments": segments, "gains": gains, "biases": biases, "qkv_weight": qkv_weight, "qv_bias": qv_bias, "out_weight": out_weight, "out_bias": out_bias, "up_weight": up_weight, "up_bias": up_bias, "down_weight": down_weight, "down_bias": down_bias}


eps = 1e-05

@jax.custom_vjp
def low(v):
    return lax.optimization_barrier(v.astype(jnp.bfloat16)).astype(jnp.float32)

@jax.custom_vjp
def low_back(v):
    return v

def low_keep(v):
    return (low(v), None)

def low_pass(kept, grad):
    return (grad,)

def back_keep(v):
    return (v, None)

def back_low(kept, grad):
    return (low(grad),)
low.defvjp(low_keep, low_pass)
low_back.defvjp(back_keep, back_low)

def layer_norm(values_in, gain, bias):
    centre = lax.optimization_barrier(jnp.mean(values_in, axis=-1, keepdims=True))
    centred = values_in - centre
    variance = lax.optimization_barrier(jnp.mean(centred * centred, axis=-1, keepdims=True))
    return centred * lax.rsqrt(variance + eps) * gain + bias

def matmul(left, right):
    return jnp.dot(left, right, precision=lax.Precision.HIGHEST, preferred_element_type=jnp.float32)

def one_head(inputs, segment_ids):
    queries, keys, values, slope = inputs
    places = jnp.arange(SEQ, dtype=jnp.int32)
    distance = (places[:, None] - places[None, :]).astype(jnp.float32)
    raw = matmul(queries, keys.T) * HD ** (-0.5)
    raw = raw - slope * distance
    allowed = (places[None, :] <= places[:, None]) & (segment_ids[:, None] == segment_ids[None, :])
    scores = low_back(jnp.where(allowed, raw, -1e+30))
    highest = lax.optimization_barrier(jnp.max(scores, axis=-1, keepdims=True))
    shifted = jnp.exp(scores - highest)
    chances = low(shifted / lax.optimization_barrier(jnp.sum(shifted, axis=-1, keepdims=True)))
    return matmul(chances, values)

def layer(hidden, weights, segment_ids, slopes):
    gain_one, bias_one, gain_two, bias_two, joined_weight, pair_bias, out_weight, out_bias, up_weight, up_bias, down_weight, down_bias = weights
    normed = low(layer_norm(hidden, gain_one, bias_one))
    joined = matmul(normed, joined_weight).reshape(SEQ, H, 3, HD)
    queries = low(low_back(joined[:, :, 0] + pair_bias[0].reshape(H, HD)))
    keys = low(low_back(joined[:, :, 1]))
    values = low(low_back(joined[:, :, 2] + pair_bias[1].reshape(H, HD)))
    checked = jax.checkpoint(partial(one_head, segment_ids=segment_ids))
    heads = lax.map(checked, (jnp.transpose(queries, (1, 0, 2)), jnp.transpose(keys, (1, 0, 2)), jnp.transpose(values, (1, 0, 2)), slopes))
    context = low(low_back(jnp.transpose(heads, (1, 0, 2)).reshape(SEQ, D)))
    middle = hidden + low_back(matmul(context, out_weight)) + out_bias
    spread = low(layer_norm(middle, gain_two, bias_two))
    pre = low_back(matmul(spread, up_weight) + up_bias)
    active = low(jax.nn.gelu(pre, approximate=True))
    return middle + low_back(matmul(active, down_weight)) + down_bias

def section_weights(params, index):
    gains, biases, joined, pair, out_weight, out_bias, up_weight, up_bias, down_weight, down_bias = params
    return (gains[index, 1], biases[index, 1], gains[index, 2], biases[index, 2], joined[index], pair[index], out_weight[index], out_bias[index], up_weight[index], up_bias[index], down_weight[index], down_bias[index])

def forward_row(entry, params, segment_ids, slopes):
    gains, biases = (params[0], params[1])
    start = layer_norm(entry, gains[0, 0], biases[0, 0])
    middle_out = layer(start, section_weights(params, 0), segment_ids, slopes)
    passed = low(low_back(middle_out))
    last = layer(passed, section_weights(params, 1), segment_ids, slopes)
    return layer_norm(last, gains[1, 0], biases[1, 0])

def reference(boundary, segments, gains, biases, qkv_weight, qv_bias, out_weight, out_bias, up_weight, up_bias, down_weight, down_bias):
    params = tuple((item.astype(jnp.float32) for item in (gains, biases, qkv_weight, qv_bias, out_weight, out_bias, up_weight, up_bias, down_weight, down_bias)))
    slopes = jnp.exp2(-8.0 * jnp.arange(1, H + 1, dtype=jnp.float32) / H)
    entries = boundary[0].astype(jnp.float32).reshape(MB * ROWS, SEQ, D)
    cotangents = boundary[1].astype(jnp.float32).reshape(MB * ROWS, SEQ, D)
    segment_rows = segments.reshape(MB * ROWS, SEQ)

    def row_step(totals, item):
        entry, cotangent, segment_ids = item

        def run(entry_in, weights):
            return forward_row(entry_in, weights, segment_ids, slopes)
        output, pull = jax.vjp(run, entry, params)
        grad_entry, grad_params = pull(cotangent)
        totals = jax.tree.map(jnp.add, totals, grad_params)
        return (totals, (output, grad_entry))
    zeros = jax.tree.map(jnp.zeros_like, params)
    totals, (outputs, entry_grads) = lax.scan(row_step, zeros, (entries, cotangents, segment_rows))
    centred = entries - lax.optimization_barrier(jnp.mean(entries, axis=-1, keepdims=True))
    embed_stat = jnp.mean(lax.optimization_barrier(jnp.mean(centred * centred, axis=-1)))
    ends_out = jnp.stack([entry_grads, outputs]).reshape(2, MB, ROWS, SEQ, D)
    return (ends_out, embed_stat, totals[0], totals[1], totals[2], totals[3], totals[4], totals[5], totals[6], totals[7], totals[8], totals[9])
```

```python
import jax
import jax.numpy as jnp
from jax import lax
from jax.experimental import pallas as pl
from jax.experimental.pallas import tpu as pltpu
from jax.sharding import PartitionSpec as P

H = 16
HD = 64
eps = 1e-05

f32 = jnp.float32
bf16 = jnp.bfloat16


def swap_half(array):
    size = lax.axis_size("tensor")
    pairs = [(i, (i + size // 2) % size) for i in range(size)]
    return lax.ppermute(array, "tensor", pairs)


def from_rank(array, by):
    size = lax.axis_size("tensor")
    ranks = size // 2
    pairs = [
        (m * ranks + (j + by) % ranks, m * ranks + j) for m in range(2) for j in range(ranks)
    ]
    return lax.ppermute(array, "tensor", pairs)


def from_section(array, by):
    size = lax.axis_size("section")
    pairs = [(i, i + by) for i in range(size) if 0 <= i + by < size]
    return lax.ppermute(array, "section", pairs)


def gather_rows(own):
    ranks = lax.axis_size("tensor") // 2
    return [own] + [from_rank(own, k) for k in range(1, ranks)]


def scatter_sum(part_of):
    ranks = lax.axis_size("tensor") // 2
    arrived = [from_rank(part_of(k).astype(bf16), ranks - k) for k in range(1, ranks)]
    total = part_of(0)
    for part in arrived:
        total = total + part.astype(f32)
    return total


def butterfly(array, axis):
    size = lax.axis_size(axis)
    if size & (size - 1):
        return lax.psum(array, axis)
    step = 1
    while step < size:
        array = array + lax.ppermute(array, axis, [(i, i ^ step) for i in range(size)])
        step *= 2
    return array


def dot(left, right):
    return jnp.dot(left, right, preferred_element_type=f32)


def dot_nt(left, right):
    return lax.dot_general(left, right, (((1,), (1,)), ((), ())), preferred_element_type=f32)


def dot_tn(left, right):
    return lax.dot_general(left, right, (((0,), (0,)), ((), ())), preferred_element_type=f32)


def normalise(values_in):
    centre = jnp.mean(values_in, axis=-1, keepdims=True)
    centred = values_in - centre
    variance = jnp.mean(centred * centred, axis=-1, keepdims=True)
    scale = lax.rsqrt(variance + eps)
    return centred * scale, scale


def layer_norm(values_in, gain, bias):
    return normalise(values_in)[0] * gain + bias


def layer_norm_back(values_in, gain, grad):
    hat, scale = normalise(values_in)
    scaled = grad * gain
    inner = jnp.mean(scaled, axis=-1, keepdims=True)
    along = jnp.mean(scaled * hat, axis=-1, keepdims=True)
    grad_in = scale * (scaled - inner - hat * along)
    return grad_in, jnp.sum(grad * hat, axis=0), jnp.sum(grad, axis=0)


def variance_total(values_in):
    centred = values_in - jnp.mean(values_in, axis=-1, keepdims=True)
    return jnp.sum(jnp.mean(centred * centred, axis=-1))


def gelu_pair(pre):
    root = 0.7978845608028654
    square = pre * pre
    bent = jnp.tanh(root * pre * (1.0 + 0.044715 * square))
    rise = 0.5 * (1.0 + bent)
    slope = rise + 0.5 * pre * (1.0 - bent * bent) * root * (1.0 + 3 * 0.044715 * square)
    return pre * rise, slope


def attend(joined, places, segment_ids, slopes):
    heads = slopes.shape[0]
    width = heads * HD
    whole = jnp.concatenate(joined, axis=0)
    length = whole.shape[0]
    split = whole.reshape(length, 3, heads, HD).transpose(1, 2, 0, 3)
    queries, keys, values = split[0], split[1], split[2]
    raw = jnp.einsum("hqd,hkd->hqk", queries, keys, preferred_element_type=f32) * HD ** (-0.5)
    distance = (places[:, None] - places[None, :]).astype(f32)
    raw = raw - slopes[:, None, None] * distance
    allowed = (distance >= 0) & (segment_ids[:, None] == segment_ids[None, :])
    scores = jnp.where(allowed, raw, -1e30)
    highest = jnp.max(scores, axis=-1, keepdims=True)
    shifted = jnp.exp(scores - highest)
    summed = jnp.sum(shifted, axis=-1, keepdims=True)
    chances = (shifted / summed).astype(bf16)
    context = jnp.einsum("hqk,hkd->hqd", chances, values, preferred_element_type=f32)
    context = context.astype(bf16).transpose(1, 0, 2).reshape(length, width)
    log_total = highest + jnp.log(summed)
    count = len(joined)
    return jnp.split(context, count), log_total


def attend_back(joined, context, log_total, grad_context, places, segment_ids, slopes):
    heads = slopes.shape[0]
    whole = jnp.concatenate(joined, axis=0)
    length = whole.shape[0]
    split = whole.reshape(length, 3, heads, HD).transpose(1, 2, 0, 3)
    queries, keys, values = split[0], split[1], split[2]
    grad = jnp.concatenate(grad_context).reshape(length, heads, HD).transpose(1, 0, 2)
    raw = jnp.einsum("hqd,hkd->hqk", queries, keys, preferred_element_type=f32) * HD ** (-0.5)
    distance = (places[:, None] - places[None, :]).astype(f32)
    raw = raw - slopes[:, None, None] * distance
    allowed = (distance >= 0) & (segment_ids[:, None] == segment_ids[None, :])
    chances = jnp.exp(jnp.where(allowed, raw, -1e30) - log_total)
    grad_chances = jnp.einsum("hqd,hkd->hqk", grad, values, preferred_element_type=f32)
    inner = jnp.sum(chances * grad_chances, axis=-1, keepdims=True)
    grad_scores = (chances * (grad_chances - inner)).astype(bf16)
    chances = chances.astype(bf16)
    grad_q = jnp.einsum("hqk,hkd->qhd", grad_scores, keys, preferred_element_type=f32) * HD ** (-0.5)
    grad_k = jnp.einsum("hqk,hqd->khd", grad_scores, queries, preferred_element_type=f32) * HD ** (-0.5)
    grad_v = jnp.einsum("hqk,hqd->khd", chances, grad, preferred_element_type=f32)
    out = jnp.stack([grad_q, grad_k, grad_v], axis=1).astype(bf16).reshape(length, -1)
    return jnp.split(out, len(joined))


def forward(hidden, weights, places, segment_ids, slopes):
    gain_one, bias_one, gain_two, bias_two, joined_w, joined_b, out_w, out_b = weights[:8]
    up_w, up_b, down_w, down_b = weights[8:]
    normed = gather_rows(layer_norm(hidden, gain_one, bias_one).astype(bf16))
    joined = [(dot(part, joined_w) + joined_b).astype(bf16) for part in normed]
    context, log_total = attend(joined, places, segment_ids, slopes)
    middle = hidden + scatter_sum(lambda k: dot(context[k], out_w)) + out_b
    spread = gather_rows(layer_norm(middle, gain_two, bias_two).astype(bf16))
    active, bent = [], []
    for part in spread:
        act, slope = gelu_pair(dot(part, up_w) + up_b)
        active.append(act.astype(bf16))
        bent.append(slope.astype(bf16))
    result = middle + scatter_sum(lambda k: dot(active[k], down_w)) + down_b
    kept = (hidden, normed, joined, context, log_total, middle, spread, active, bent)
    return result, kept


def backward(grad, kept, weights, places, segment_ids, slopes):
    hidden, normed, joined, context, log_total, middle, spread, active, bent = kept
    gain_one, bias_one, gain_two, bias_two, joined_w, joined_b, out_w, out_b = weights[:8]
    up_w, up_b, down_w, down_b = weights[8:]
    count = len(normed)

    def over(left, right):
        return sum(dot_tn(left[k], right[k]) for k in range(count))

    grad_down_b = jnp.sum(grad, axis=0)
    grads = gather_rows(grad.astype(bf16))
    down_grad = over(active, grads)
    grad_pre = [
        (dot_nt(grads[k], down_w) * bent[k].astype(f32)).astype(bf16) for k in range(count)
    ]
    up_b_grad = sum(jnp.sum(part, axis=0, dtype=f32) for part in grad_pre)
    up_grad = over(spread, grad_pre)
    grad_spread = scatter_sum(lambda k: dot_nt(grad_pre[k], up_w))
    grad_two, gain_two_grad, bias_two_grad = layer_norm_back(middle, gain_two, grad_spread)
    grad_middle = grad + grad_two
    out_b_grad = jnp.sum(grad_middle, axis=0)
    grads = gather_rows(grad_middle.astype(bf16))
    out_grad = over(context, grads)
    grad_context = [dot_nt(part, out_w).astype(bf16) for part in grads]
    grad_joined = attend_back(
        joined, context, log_total, grad_context, places, segment_ids, slopes
    )
    joined_b_grad = sum(jnp.sum(part, axis=0, dtype=f32) for part in grad_joined)
    joined_grad = over(normed, grad_joined)
    grad_normed = scatter_sum(lambda k: dot_nt(grad_joined[k], joined_w))
    grad_one, gain_one_grad, bias_one_grad = layer_norm_back(hidden, gain_one, grad_normed)
    matrices = (joined_grad, out_grad, up_grad, down_grad)
    halves = (joined_b_grad, up_b_grad)
    shared = (
        gain_one_grad,
        bias_one_grad,
        gain_two_grad,
        bias_two_grad,
        out_b_grad,
        grad_down_b,
    )
    return grad_middle + grad_one, matrices, halves, shared


def local(
    boundary,
    segments,
    gains,
    biases,
    qkv_weight,
    qv_bias,
    out_weight,
    out_bias,
    up_weight,
    up_bias,
    down_weight,
    down_bias,
):
    first = lax.axis_index("section") == 0
    tensor = lax.axis_size("tensor")
    ranks = tensor // 2
    place = lax.axis_index("tensor")
    half, rank = place // ranks, place % ranks
    micro_count, own_rows, width = boundary.shape[1], boundary.shape[3], boundary.shape[4]
    heads = qkv_weight.shape[2] // (3 * HD)
    hidden_units = up_weight.shape[2]

    rows = boundary[0, :, 0]
    mine = jnp.where(half == 0, rows[0], rows[1])
    other = jnp.where(half == 0, rows[1], rows[0])
    own_end = jnp.concatenate([mine, swap_half(other)]).astype(f32)

    order = [(rank + k) % ranks for k in range(ranks)]
    blocks = [b for r in order for b in (half * ranks + r, (1 - half) * ranks + r)]
    places = jnp.concatenate([b * own_rows + lax.iota(jnp.int32, own_rows) for b in blocks])
    row_segments = jnp.where(half == 0, segments[0, 0], segments[1, 0])
    segment_ids = row_segments[places]
    partner = (1 - half) * ranks + rank
    head_index = jnp.concatenate(
        [p * heads + lax.iota(jnp.int32, heads) for p in (place, partner)]
    )
    slopes = jnp.exp2(-8.0 * (head_index + 1).astype(f32) / H)

    own_joined = (
        qkv_weight[0].reshape(width, heads, 3, HD).transpose(0, 2, 1, 3).reshape(width, 3, -1)
    )
    joined_w = jnp.concatenate([own_joined, swap_half(own_joined)], axis=2).reshape(width, -1)
    out_w = jnp.concatenate([out_weight[0], swap_half(out_weight[0])], axis=0)
    up_w = jnp.concatenate([up_weight[0], swap_half(up_weight[0])], axis=1)
    down_w = jnp.concatenate([down_weight[0], swap_half(down_weight[0])], axis=0)
    thin = jnp.concatenate([qv_bias[0].reshape(-1), up_bias[0]])
    thin_other = swap_half(thin)
    pair = qv_bias.shape[2]
    joined_b = jnp.concatenate(
        [
            thin[:pair],
            thin_other[:pair],
            jnp.zeros((2 * pair,), f32),
            thin[pair : 2 * pair],
            thin_other[pair : 2 * pair],
        ]
    )
    up_b = jnp.concatenate([thin[2 * pair :], thin_other[2 * pair :]])
    weights = (
        gains[0, 1],
        biases[0, 1],
        gains[0, 2],
        biases[0, 2],
        joined_w,
        joined_b,
        out_w,
        out_bias[0],
        up_w,
        up_b,
        down_w,
        down_bias[0],
    )

    spread_total = jnp.where(first, variance_total(rows.astype(f32)), 0.0)
    token_count = micro_count * own_rows * tensor * lax.axis_size("dp")
    stat = jnp.broadcast_to(spread_total, (1, 128))
    for axis in ("tensor", "dp", "section"):
        stat = butterfly(stat, axis)
    embed_stat = stat[0, 0] / token_count

    start = layer_norm(own_end, gains[0, 0], biases[0, 0])
    result, _ = forward(start, weights, places, segment_ids, slopes)
    passed = from_section(result.astype(bf16), 1).astype(f32)
    result, kept = forward(jnp.where(first, start, passed), weights, places, segment_ids, slopes)
    final = layer_norm(result, gains[0, 0], biases[0, 0])

    grad_last, gain_last, bias_last = layer_norm_back(result, gains[0, 0], own_end)
    grad_passed = backward(grad_last, kept, weights, places, segment_ids, slopes)[0]
    arrived = from_section(grad_passed.astype(bf16), -1).astype(f32)
    grad = jnp.where(first, arrived, grad_last)
    grad_start, matrices, halves, shared = backward(
        grad, kept, weights, places, segment_ids, slopes
    )
    grad_entry, gain_first, bias_first = layer_norm_back(own_end, gains[0, 0], grad_start)

    ends = jnp.where(first, grad_entry, final)
    ends_mine = ends[:own_rows]
    ends_other = swap_half(ends[own_rows:].astype(bf16)).astype(f32)
    ends_out = jnp.stack(
        [
            jnp.where(half == 0, ends_mine, ends_other),
            jnp.where(half == 0, ends_other, ends_mine),
        ]
    )[None, :, None]

    joined_grad, out_grad, up_grad, down_grad = matrices
    joined_grad = joined_grad.reshape(width, 3, 2, heads, HD).transpose(2, 0, 3, 1, 4)
    joined_grad = joined_grad.reshape(2, width, -1)
    out_grad = out_grad.reshape(2, -1, width)
    up_grad = up_grad.reshape(width, 2, hidden_units).transpose(1, 0, 2)
    down_grad = down_grad.reshape(2, hidden_units, width)

    def summed(pair_grad):
        total = pair_grad[0] + swap_half(pair_grad[1].astype(bf16)).astype(f32)
        return lax.psum(total.astype(bf16), "dp").astype(f32)

    down_grad, up_grad, out_grad, joined_grad = [
        summed(part) for part in (down_grad, up_grad, out_grad, joined_grad)
    ]

    joined_b_grad, up_b_grad = halves
    joined_b_grad = joined_b_grad.reshape(3, 2, pair)
    up_b_grad = up_b_grad.reshape(2, hidden_units)
    thin_grads = [
        jnp.concatenate([joined_b_grad[0, k], joined_b_grad[2, k], up_b_grad[k]]) for k in range(2)
    ]
    thin_grad = thin_grads[0] + swap_half(thin_grads[1])
    shared = jnp.stack(
        [jnp.where(first, gain_first, gain_last), jnp.where(first, bias_first, bias_last), *shared]
    )
    shared = butterfly(shared, "tensor")
    flat = butterfly(jnp.concatenate([shared.reshape(-1), thin_grad]), "dp")
    shared = flat[: 8 * width].reshape(8, width)
    thin_grad = flat[8 * width :]
    gain_grads = jnp.stack([shared[0], shared[2], shared[4]])[None]
    bias_grads = jnp.stack([shared[1], shared[3], shared[5]])[None]
    return (
        ends_out,
        embed_stat,
        gain_grads,
        bias_grads,
        joined_grad[None],
        thin_grad[: 2 * pair].reshape(1, 2, pair),
        out_grad[None],
        shared[6][None],
        up_grad[None],
        thin_grad[2 * pair :][None],
        down_grad[None],
        shared[7][None],
    )


def solution(mesh):
    return jax.shard_map(
        local,
        mesh=mesh,
        in_specs=(
            P("section", None, "dp", "tensor", None),
            P(None, "dp", None),
            P("section", None, None),
            P("section", None, None),
            P("section", None, "tensor"),
            P("section", None, "tensor"),
            P("section", "tensor", None),
            P("section", None),
            P("section", None, "tensor"),
            P("section", "tensor"),
            P("section", "tensor", None),
            P("section", None),
        ),
        out_specs=(
            P("section", None, "dp", "tensor", None),
            P(),
            P("section", None, None),
            P("section", None, None),
            P("section", None, "tensor"),
            P("section", None, "tensor"),
            P("section", "tensor", None),
            P("section", None),
            P("section", None, "tensor"),
            P("section", "tensor"),
            P("section", "tensor", None),
            P("section", None),
        ),
        check_vma=False,
    )
```

```python
from functools import partial

import jax
import jax.numpy as jnp
from jax import lax
from jax.experimental import pallas as pl
from jax.experimental.pallas import tpu as pltpu
from jax.sharding import PartitionSpec as P

H = 16
HD = 64
eps = 1e-05

f32 = jnp.float32
bf16 = jnp.bfloat16

MIB = 1024 * 1024


def swap_half(array):
    size = lax.axis_size("tensor")
    pairs = [(i, (i + size // 2) % size) for i in range(size)]
    return lax.ppermute(array, "tensor", pairs)


def from_rank(array, by):
    size = lax.axis_size("tensor")
    ranks = size // 2
    pairs = [
        (m * ranks + (j + by) % ranks, m * ranks + j) for m in range(2) for j in range(ranks)
    ]
    return lax.ppermute(array, "tensor", pairs)


def from_section(array, by):
    size = lax.axis_size("section")
    pairs = [(i, i + by) for i in range(size) if 0 <= i + by < size]
    return lax.ppermute(array, "section", pairs)


def gather_rows(own):
    ranks = lax.axis_size("tensor") // 2
    return [own] + [from_rank(own, k) for k in range(1, ranks)]


def scatter_sum(part_of):
    ranks = lax.axis_size("tensor") // 2
    arrived = [from_rank(part_of(k).astype(bf16), ranks - k) for k in range(1, ranks)]
    total = part_of(0)
    for part in arrived:
        total = total + part.astype(f32)
    return total


def butterfly(array, axis, parts=1):
    size = lax.axis_size(axis)
    step = 1
    while step < size // parts:
        array = array + lax.ppermute(array, axis, [(i, i ^ step) for i in range(size)])
        step *= 2
    return array


def ring_pass(share, axis):
    size = lax.axis_size(axis)
    ring = [(i, (i + 1) % size) for i in range(size)]
    shares = [share]
    for _ in range(size - 1):
        shares.append(lax.ppermute(shares[-1], axis, ring))
    return shares


def after(array, *others):
    return lax.optimization_barrier((array, *others))[0]


def plus(one, two):
    return (one.astype(f32) + two.astype(f32)).astype(bf16)


class RowSums:
    ends = [(0, 1), (1, 0), (2, 3), (3, 2)]
    centre = [(1, 2), (2, 1)]

    def __init__(self, axis):
        self.axis = axis
        self.line = lax.axis_size(axis) == 4
        place = lax.axis_index(axis)
        self.outer = (place == 0) | (place == 3)
        self.tasks, self.ready = [], []
        self.swapped, self.chunks, self.partials, self.totals = [], [], [], []
        self.from_end, self.from_centre = [], []

    def prepare(self, *others):
        if len(self.ready) < len(self.tasks):
            task = self.tasks[len(self.ready)]
            fence = (lambda array: after(array, *others)) if others else lambda array: array
            parts = [task(at, fence).astype(bf16) for at in (1, 0)]
            self.ready.append(lax.optimization_barrier(parts))

    def swap(self, *others):
        if len(self.swapped) < len(self.ready):
            part = self.ready[len(self.swapped)][0]
            self.swapped.append(swap_half(after(part, *others) if others else part))

    def step(self, *others):
        step = len(self.from_end)
        come = self.swapped[-1:] + self.from_end[-1:] + self.from_centre[-1:] + list(others)
        if step < len(self.tasks):
            self.chunks.append(plus(self.ready[step][1], self.swapped[step]))
        if not self.line:
            self.from_end.append(None)
            come = self.swapped[-1:]
        else:
            if 0 <= step - 1 < len(self.chunks):
                self.partials.append(plus(self.chunks[step - 1], self.from_end[step - 1]))
            if step >= 2:
                self.totals.append(plus(self.partials[step - 2], self.from_centre[step - 2]))
            if step >= len(self.tasks):
                to_end = self.totals[step - 2]
            elif step >= 2:
                fresh, done = self.chunks[step], self.totals[step - 2]
                done = jnp.pad(done, ((0, fresh.shape[0] - done.shape[0]), (0, 0)))
                to_end = jnp.where(self.outer, fresh, done)
            else:
                to_end = self.chunks[step]
            self.from_end.append(lax.ppermute(after(to_end, *come), self.axis, self.ends))
            if 0 <= step - 1 < len(self.chunks):
                middle = after(self.partials[step - 1], *come)
                self.from_centre.append(lax.ppermute(middle, self.axis, self.centre))
        self.swap(*come)
        self.prepare(*come)
        return come

    def finish(self):
        count = len(self.tasks)
        while len(self.from_end) < count + 2:
            self.step()
        if not self.line:
            return [lax.psum(chunk, self.axis) for chunk in self.chunks]
        back = [self.from_end[n + 2][: self.totals[n].shape[0]] for n in range(count)]
        return [jnp.where(self.outer, back[n], self.totals[n]) for n in range(count)]


def dot(left, right):
    return jnp.dot(left, right, preferred_element_type=f32)


def dot_nt(left, right):
    return lax.dot_general(left, right, (((1,), (1,)), ((), ())), preferred_element_type=f32)


def dot_tn(left, right):
    return lax.dot_general(left, right, (((0,), (0,)), ((), ())), preferred_element_type=f32)


def normalise(values_in):
    centre = jnp.mean(values_in, axis=-1, keepdims=True)
    centred = values_in - centre
    variance = jnp.mean(centred * centred, axis=-1, keepdims=True)
    scale = lax.rsqrt(variance + eps)
    return centred * scale, scale


def layer_norm(values_in, gain, bias):
    return normalise(values_in)[0] * gain + bias


def layer_norm_back(values_in, gain, grad):
    hat, scale = normalise(values_in)
    scaled = grad * gain
    inner = jnp.mean(scaled, axis=-1, keepdims=True)
    along = jnp.mean(scaled * hat, axis=-1, keepdims=True)
    grad_in = scale * (scaled - inner - hat * along)
    return grad_in, jnp.sum(grad * hat, axis=0), jnp.sum(grad, axis=0)


def variance_total(values_in):
    centred = values_in - jnp.mean(values_in, axis=-1, keepdims=True)
    return jnp.sum(jnp.mean(centred * centred, axis=-1))


def gelu_pair(pre):
    root = 0.7978845608028654
    square = pre * pre
    bent = jnp.tanh(root * pre * (1.0 + 0.044715 * square))
    rise = 0.5 * (1.0 + bent)
    slope = rise + 0.5 * pre * (1.0 - bent * bent) * root * (1.0 + 3 * 0.044715 * square)
    return pre * rise, slope


def fetch(scratch, pieces, blocks_ref, rows, scale=None):
    slots = pieces[0].shape[0] // rows
    for b in range(len(pieces) * slots):
        part = pieces[b // slots][pl.ds((b % slots) * rows, rows), :]
        if scale is not None:
            part = part * scale
        scratch[pl.ds(pl.multiple_of(blocks_ref[b] * rows, rows), rows), :] = part


def only_head(values, e):
    lane = lax.broadcasted_iota(jnp.int32, values.shape, 1)
    return jnp.where((lane >= HD) == (e == 1), values, jnp.zeros_like(values))


def fill_distance(far, seg_col_ref, seg_row_ref, rows, flipped):
    length = far.shape[0]
    for one in range(length // rows):
        for two in range(one + 1):
            low, high = pl.ds(one * rows, rows), pl.ds(two * rows, rows)
            if flipped:
                low, high = high, low
            shape = (rows, rows)
            along = lax.broadcasted_iota(jnp.int32, shape, 0) - lax.broadcasted_iota(
                jnp.int32, shape, 1
            )
            gap = (-along if flipped else along) + (one - two) * rows
            same = seg_col_ref[low, :] == seg_row_ref[:, high]
            far[low, high] = jnp.where(same & (gap >= 0), gap.astype(f32), 1e32)


def attend_kernel(count, rows, blocks_ref, slopes_ref, seg_col_ref, seg_row_ref, *refs):
    q_in, k_in, v_in = refs[:count], refs[count : 2 * count], refs[2 * count : 3 * count]
    context_out = refs[3 * count : 4 * count]
    log_out = refs[4 * count]
    queries, keys, values, context, far = refs[4 * count + 1 :]
    pair = pl.program_id(0)
    length = queries.shape[0]

    @pl.when(pair == 0)
    def _():
        fill_distance(far, seg_col_ref, seg_row_ref, rows, False)

    fetch(queries, q_in, blocks_ref, rows, jnp.asarray(HD**-0.5, bf16))
    fetch(keys, k_in, blocks_ref, rows)
    fetch(values, v_in, blocks_ref, rows)
    lane = lax.broadcasted_iota(jnp.int32, (rows, 128), 1)
    for i in range(length // rows):
        here, until = pl.ds(i * rows, rows), pl.ds(0, (i + 1) * rows)
        total = None
        logs = None
        for e in range(2):
            slope = slopes_ref[2 * pair + e]
            scores = dot_nt(only_head(queries[here, :], e), keys[until, :])
            scores = scores - slope * far[here, until]
            highest = jnp.max(scores, axis=1, keepdims=True)
            shifted = jnp.exp(scores - highest)
            summed = jnp.sum(shifted, axis=1, keepdims=True)
            part = dot(shifted.astype(bf16), only_head(values[until, :], e)) / summed
            log = highest + jnp.log(summed)
            total = part if e == 0 else total + part
            logs = jnp.broadcast_to(log, (rows, 128)) if e == 0 else jnp.where(lane == 1, log, logs)
        context[here, :] = total.astype(bf16)
        log_out[0, :, here] = logs.T[:8]
    slots = q_in[0].shape[0] // rows
    for b in range(count * slots):
        context_out[b // slots][pl.ds((b % slots) * rows, rows), :] = context[
            pl.ds(pl.multiple_of(blocks_ref[b] * rows, rows), rows), :
        ]


def attend_back_kernel(count, rows, blocks_ref, slopes_ref, seg_col_ref, seg_row_ref, *refs):
    q_in, k_in, v_in, c_in, g_in = [refs[n * count : (n + 1) * count] for n in range(5)]
    log_in = refs[5 * count]
    grad_out = refs[5 * count + 1 : 6 * count + 1]
    queries, keys, values, context, grads, far, grad_q, grad_k, grad_v = refs[6 * count + 1 :]
    pair = pl.program_id(0)
    length = queries.shape[0]
    width = grad_out[0].shape[1] // 3

    @pl.when(pair == 0)
    def _():
        fill_distance(far, seg_col_ref, seg_row_ref, rows, True)

    fetch(queries, q_in, blocks_ref, rows, jnp.asarray(HD**-0.5, bf16))
    fetch(keys, k_in, blocks_ref, rows)
    fetch(values, v_in, blocks_ref, rows)
    fetch(context, c_in, blocks_ref, rows)
    fetch(grads, g_in, blocks_ref, rows)
    head_of = lax.broadcasted_iota(jnp.int32, (8, 128), 1) // HD
    chosen = (head_of == lax.broadcasted_iota(jnp.int32, (8, 128), 0)).astype(f32)
    inner = lax.dot_general(
        chosen,
        context[...].astype(f32) * grads[...].astype(f32),
        (((1,), (1,)), ((), ())),
        precision=lax.Precision.HIGHEST,
        preferred_element_type=f32,
    )
    grad_k[...] = jnp.zeros_like(grad_k)
    grad_v[...] = jnp.zeros_like(grad_v)
    for i in range(length // rows):
        here, until = pl.ds(i * rows, rows), pl.ds(0, (i + 1) * rows)
        chances, slants, heads_q, heads_g, heads_k = [], [], [], [], []
        for e in range(2):
            slope = slopes_ref[2 * pair + e]
            query = only_head(queries[here, :], e)
            grad = only_head(grads[here, :], e)
            scores = dot_nt(keys[until, :], query)
            scores = scores - slope * far[until, here] - log_in[0, e : e + 1, here]
            chance = jnp.exp(scores)
            grad_chance = dot_nt(values[until, :], grad)
            slant = chance * (grad_chance - inner[e : e + 1, i * rows : (i + 1) * rows])
            chances.append(chance.astype(bf16))
            slants.append(slant.astype(bf16))
            heads_q.append(query)
            heads_g.append(grad)
            heads_k.append(only_head(keys[until, :], e))
        grad_v[until, :] += dot(jnp.concatenate(chances, axis=1), jnp.concatenate(heads_g, axis=0))
        grad_k[until, :] += dot(jnp.concatenate(slants, axis=1), jnp.concatenate(heads_q, axis=0))
        grad_q[here, :] = (
            dot_tn(slants[0], heads_k[0]) + dot_tn(slants[1], heads_k[1])
        ) * HD**-0.5
    slots = q_in[0].shape[0] // rows
    for b in range(count * slots):
        place = pl.ds(pl.multiple_of(blocks_ref[b] * rows, rows), rows)
        for n, part in enumerate((grad_q, grad_k, grad_v)):
            column = pl.ds(pl.multiple_of(n * width + pair * 128, 128), 128)
            grad_out[b // slots][pl.ds((b % slots) * rows, rows), column] = part[place, :].astype(
                bf16
            )


def attention_specs(joined, segment_ids):
    count, rows_of_piece = len(joined), joined[0].shape[0]
    pairs = joined[0].shape[1] // (3 * 128)
    length = segment_ids.shape[0]
    smem = pl.BlockSpec(memory_space=pltpu.SMEM)
    common = [
        smem,
        smem,
        pl.BlockSpec((length, 1), lambda p: (0, 0)),
        pl.BlockSpec((1, length), lambda p: (0, 0)),
    ]

    def column(n):
        return pl.BlockSpec((rows_of_piece, 128), lambda p: (0, n * pairs + p))

    log_spec = pl.BlockSpec((1, 8, length), lambda p: (p, 0, 0))
    return count, rows_of_piece, pairs, length, common, column, log_spec


def attend(joined, order, segment_ids, slopes):
    count, piece, pairs, length, common, column, log_spec = attention_specs(joined, segment_ids)
    rows = length // order.shape[0]
    low = pltpu.VMEM((length, 128), bf16)
    out = pl.pallas_call(
        partial(attend_kernel, count, rows),
        grid=(pairs,),
        in_specs=common + [column(n) for n in range(3) for _ in range(count)],
        out_specs=[column(0)] * count + [log_spec],
        out_shape=[jax.ShapeDtypeStruct((piece, pairs * 128), bf16)] * count
        + [jax.ShapeDtypeStruct((pairs, 8, length), f32)],
        scratch_shapes=[low, low, low, low, pltpu.VMEM((length, length), f32)],
        compiler_params=pltpu.CompilerParams(vmem_limit_bytes=16 * MIB),
        cost_estimate=pl.CostEstimate(
            flops=pairs * 128 * length,
            bytes_accessed=length * pairs * 128,
            transcendentals=0,
        ),
        name="attend",
    )(order, slopes, segment_ids[:, None], segment_ids[None], *joined, *joined, *joined)
    return out[:count], out[count]


def attend_back(joined, context, logs, grad_context, order, segment_ids, slopes):
    count, piece, pairs, length, common, column, log_spec = attention_specs(joined, segment_ids)
    rows = length // order.shape[0]
    low, high = pltpu.VMEM((length, 128), bf16), pltpu.VMEM((length, 128), f32)
    whole = pl.BlockSpec((piece, 3 * pairs * 128), lambda p: (0, 0))
    out = pl.pallas_call(
        partial(attend_back_kernel, count, rows),
        grid=(pairs,),
        in_specs=common
        + [column(n) for n in range(3) for _ in range(count)]
        + [column(0)] * (2 * count)
        + [log_spec],
        out_specs=[whole] * count,
        out_shape=[jax.ShapeDtypeStruct((piece, 3 * pairs * 128), bf16)] * count,
        scratch_shapes=[low] * 5 + [pltpu.VMEM((length, length), f32)] + [high] * 3,
        compiler_params=pltpu.CompilerParams(vmem_limit_bytes=28 * MIB),
        cost_estimate=pl.CostEstimate(
            flops=pairs * 128 * length,
            bytes_accessed=length * pairs * 128,
            transcendentals=0,
        ),
        name="attend_back",
    )(
        order,
        slopes,
        segment_ids[:, None],
        segment_ids[None],
        *joined,
        *joined,
        *joined,
        *context,
        *grad_context,
        logs,
    )
    return out


def forward(hidden, weights, places, segment_ids, groups):
    gain_one, bias_one, gain_two, bias_two, _, _, _, out_b, up_w, up_b, down_w, down_b = weights
    normed = gather_rows(layer_norm(hidden, gain_one, bias_one).astype(bf16))
    parts = []
    for joined_w, joined_b, out_w, slopes in groups:
        if parts:
            joined_b = after(joined_b, parts[-1][0][0])
        joined = [(dot(part, joined_w) + joined_b).astype(bf16) for part in normed]
        context, log_total = attend(joined, places, segment_ids, slopes)
        parts.append((context, out_w))
    middle = (
        hidden
        + scatter_sum(lambda k: sum(dot(context[k], out_w) for context, out_w in parts))
        + out_b
    )
    spread = gather_rows(layer_norm(middle, gain_two, bias_two).astype(bf16))
    active, bent = [], []
    for part in spread:
        act, slope = gelu_pair(dot(part, up_w) + up_b)
        act, slope = lax.optimization_barrier((act.astype(bf16), slope.astype(bf16)))
        active.append(act)
        bent.append(slope)
    result = middle + scatter_sum(lambda k: dot(active[k], down_w)) + down_b
    kept = (hidden, normed, joined, context, log_total, middle, spread, active, bent)
    return result, kept


def backward(grad, kept, weights, places, segment_ids, slopes, sums):
    hidden, normed, joined, context, log_total, middle, spread, active, bent = kept
    gain_one, bias_one, gain_two, bias_two, joined_w, joined_b, out_w, out_b = weights[:8]
    up_w, up_b, down_w, down_b = weights[8:]
    count = len(normed)

    grad_down_b = jnp.sum(grad, axis=0)
    grads = gather_rows(grad.astype(bf16))
    rows, units, width = out_w.shape[0] // 2, down_w.shape[0] // 2, out_w.shape[1]
    tasks = sums.tasks if sums else []
    whole_active, whole_grads = jnp.concatenate(active), jnp.concatenate(grads)
    for c in range(0, units, 2 * rows):
        tasks.append(
            lambda at, fence, c=c: dot_tn(
                whole_active[:, at * units + c : at * units + c + 2 * rows], fence(whole_grads)
            )
        )
    if sums:
        sums.prepare()
        sums.swap()
        sums.prepare()
    grad_pre = [
        lax.optimization_barrier(
            (dot_nt(grads[k], down_w) * bent[k].astype(f32)).astype(bf16)
        )
        for k in range(count)
    ]
    up_b_grad = sum(jnp.sum(part, axis=0, dtype=f32) for part in grad_pre)
    whole_spread, whole_pre = jnp.concatenate(spread), jnp.concatenate(grad_pre)
    high = 2 * rows * width // units
    for c in range(0, width, high):
        tasks.append(
            lambda at, fence, c=c: dot_tn(
                fence(whole_spread)[:, c : c + high], whole_pre[:, at * units : (at + 1) * units]
            ).reshape(2 * rows, width)
        )
    grad_spread = scatter_sum(lambda k: dot_nt(grad_pre[k], up_w))
    grad_two, gain_two_grad, bias_two_grad = layer_norm_back(middle, gain_two, grad_spread)
    grad_middle = grad + grad_two
    out_b_grad = jnp.sum(grad_middle, axis=0)
    grads = gather_rows(grad_middle.astype(bf16))
    if sums:
        sums.prepare()
        sums.prepare()
        sums.step()
        grads[0] = after(grads[0], sums.chunks[0])
    grad_context = [dot_nt(part, out_w).astype(bf16) for part in grads]
    grad_joined = attend_back(
        joined, context, log_total, grad_context, places, segment_ids, slopes
    )
    if sums:
        come = sums.step(grad_joined[0])
        grad_joined = [after(part, *come) for part in grad_joined]
    joined_b_grad = sum(jnp.sum(part, axis=0, dtype=f32) for part in grad_joined)
    whole_context, whole_middle = jnp.concatenate(context), jnp.concatenate(grads)
    whole_normed, whole_joined = jnp.concatenate(normed), jnp.concatenate(grad_joined)

    def of_joined(n, at, fence):
        first = (2 * n + at) * rows
        return dot_tn(whole_joined[:, first : first + rows], fence(whole_normed)).astype(bf16)

    def of_out(at, fence):
        left = whole_context[:, at * rows : (at + 1) * rows]
        return dot_tn(left, fence(whole_middle)).astype(bf16)

    tasks.append(
        lambda at, fence: jnp.concatenate([of_out(at, fence), of_joined(0, at, fence)])
    )
    last_parts = lambda at, fence: [of_joined(1, at, fence), of_joined(2, at, fence)]
    grad_normed = scatter_sum(lambda k: dot_nt(grad_joined[k], joined_w))
    grad_one, gain_one_grad, bias_one_grad = layer_norm_back(hidden, gain_one, grad_normed)
    halves = (joined_b_grad, up_b_grad)
    shared = (
        gain_one_grad,
        bias_one_grad,
        gain_two_grad,
        bias_two_grad,
        out_b_grad,
        grad_down_b,
    )
    return grad_middle + grad_one, last_parts, halves, shared


def local(
    boundary,
    segments,
    gains,
    biases,
    qkv_weight,
    qv_bias,
    out_weight,
    out_bias,
    up_weight,
    up_bias,
    down_weight,
    down_bias,
):
    first = lax.axis_index("section") == 0
    tensor = lax.axis_size("tensor")
    ranks = tensor // 2
    place = lax.axis_index("tensor")
    half, rank = place // ranks, place % ranks
    micro_count, own_rows, width = boundary.shape[1], boundary.shape[3], boundary.shape[4]
    heads = qkv_weight.shape[2] // (3 * HD)
    hidden_units = up_weight.shape[2]

    rows = boundary[0, :, 0]
    mine = jnp.where(half == 0, rows[0], rows[1])
    other = jnp.where(half == 0, rows[1], rows[0])

    order = [(rank + k) % ranks for k in range(ranks)]
    blocks = [b for r in order for b in (half * ranks + r, (1 - half) * ranks + r)]
    places = jnp.stack(blocks)
    segment_ids = jnp.where(half == 0, segments[0, 0], segments[1, 0])
    partner = (1 - half) * ranks + rank
    head_index = jnp.concatenate(
        [p * heads + lax.iota(jnp.int32, heads) for p in (place, partner)]
    )
    slopes = jnp.exp2(-8.0 * (head_index + 1).astype(f32) / H)

    def share(array, row=0):
        part = (array.shape[1] - row) // lax.axis_size("dp")
        at = row + lax.axis_index("dp") * part
        return lax.dynamic_slice(array, (0, at, 0), (1, part, array.shape[2]))[0]

    def arrange(joined):
        return joined.reshape(-1, heads, 3, HD).transpose(0, 2, 1, 3).reshape(joined.shape)

    up_rows, down_rows = width // 2, hidden_units // 2
    own_share = arrange(share(qkv_weight))
    joined_share = swap_half(own_share)
    thin = jnp.concatenate([qv_bias[0].reshape(-1), up_bias[0]])
    pair = qv_bias.shape[2]
    pieces, rest = [], thin
    for _ in range(3):
        pieces.append(lax.reduce_precision(rest, 8, 7))
        rest = rest - pieces[-1]
    pieces = jnp.concatenate(pieces).astype(bf16)
    thin_lines = -(-pieces.size // (16 * width)) * 16
    pieces = jnp.pad(pieces, (0, thin_lines * width - pieces.size)).reshape(thin_lines, width)
    mixed = swap_half(after(jnp.concatenate([other, out_weight[0], pieces]), own_share))
    other_end, other_out = mixed[:own_rows], mixed[own_rows:-thin_lines]
    pieces = mixed[-thin_lines:].reshape(-1)[: 3 * thin.size].reshape(3, -1).astype(f32)
    thin_other = pieces[0] + pieces[1] + pieces[2]
    up_piece, down_piece = share(up_weight, up_rows), share(down_weight, down_rows)
    up_lines = up_piece.size // width
    mixed_share = swap_half(
        after(jnp.concatenate([up_piece.reshape(-1, width), down_piece]), own_share)
    )
    up_direct = up_weight[0, :up_rows].reshape(-1, width)
    direct = swap_half(
        after(jnp.concatenate([up_direct, down_weight[0, :down_rows]]), joined_share)
    )
    other_up = direct[: up_direct.shape[0]].reshape(up_rows, hidden_units)
    other_down = direct[up_direct.shape[0] :]
    own_joined = arrange(qkv_weight[0])

    def passed_round(shares, whole, row, column):
        for step, part in enumerate(shares):
            at = (lax.axis_index("dp") - step) % len(shares)
            whole = lax.dynamic_update_slice(whole, part, (row + at * part.shape[0], column))
        return whole

    none = jnp.zeros((), bf16)
    joined_shares = ring_pass(joined_share, "dp")
    nearly = joined_shares[-2]
    mixed_shares = ring_pass(after(mixed_share, nearly), "dp")
    up_shares = [part[:up_lines].reshape(-1, hidden_units) for part in mixed_shares]
    down_shares = [part[up_lines:] for part in mixed_shares]
    other_joined = passed_round(joined_shares, jnp.zeros_like(own_joined), 0, 0)
    other_out = after(other_out, mixed_shares[1])
    up_w = jnp.pad(other_up, ((0, width - up_rows), (0, 0)))
    up_w = jnp.concatenate([up_weight[0], passed_round(up_shares, up_w, up_rows, 0)], axis=1)
    down_w = jnp.concatenate([down_weight[0], other_down])
    down_w = jnp.pad(down_w, ((0, hidden_units - down_rows), (0, 0)))
    down_w = passed_round(down_shares, down_w, hidden_units + down_rows, 0)
    other_joined, other_out, up_w, down_w = [
        lax.optimization_barrier(part) for part in (other_joined, other_out, up_w, down_w)
    ]
    joined_w = jnp.concatenate(
        [own_joined.reshape(width, 3, -1), other_joined.reshape(width, 3, -1)], axis=2
    ).reshape(width, -1)
    out_w = jnp.concatenate([out_weight[0], other_out], axis=0)
    joined_w, out_w = [lax.optimization_barrier(part) for part in (joined_w, out_w)]
    own_end = jnp.concatenate([mine, after(other_end, nearly)]).astype(f32)
    nothing = jnp.zeros((pair,), f32)
    own_b = jnp.concatenate([thin[:pair], nothing, thin[pair : 2 * pair]])
    own_b = after(own_b, nearly)
    other_b = jnp.concatenate([thin_other[:pair], nothing, thin_other[pair : 2 * pair]])
    joined_b = jnp.concatenate([own_b.reshape(3, -1), other_b.reshape(3, -1)], axis=1).reshape(-1)
    up_b = jnp.concatenate([thin[2 * pair :], thin_other[2 * pair :]])
    weights = (
        gains[0, 1],
        biases[0, 1],
        gains[0, 2],
        biases[0, 2],
        joined_w,
        joined_b,
        out_w,
        out_bias[0],
        up_w,
        up_b,
        down_w,
        down_bias[0],
    )

    start = layer_norm(own_end, gains[0, 0], biases[0, 0])
    groups = (
        (own_joined, own_b, out_weight[0], slopes[:heads]),
        (other_joined, other_b, other_out, slopes[heads:]),
    )
    result = forward(start, weights, places, segment_ids, groups)[0]
    passed = from_section(result.astype(bf16), 1).astype(f32)
    groups = ((joined_w, joined_b, out_w, slopes),)
    result, kept = forward(jnp.where(first, start, passed), weights, places, segment_ids, groups)
    final = layer_norm(result, gains[0, 0], biases[0, 0])

    spread_total = jnp.where(first, variance_total(rows.astype(f32)), 0.0)
    token_count = micro_count * own_rows * tensor * lax.axis_size("dp")
    stat = butterfly(jnp.broadcast_to(spread_total, (1, 128)), "section")
    for axis in ("tensor", "dp"):
        stat = butterfly(stat, axis)
    embed_stat = stat[0, 0] / token_count

    grad_last, gain_last, bias_last = layer_norm_back(result, gains[0, 0], own_end)
    grad_passed = backward(grad_last, kept, weights, places, segment_ids, slopes, None)[0]
    arrived = from_section(grad_passed.astype(bf16), -1).astype(f32)
    grad = jnp.where(first, arrived, grad_last)
    sums = RowSums("dp")
    grad_start, last_parts, halves, shared = backward(
        grad, kept, weights, places, segment_ids, slopes, sums
    )
    grad_entry, gain_first, bias_first = layer_norm_back(own_end, gains[0, 0], grad_start)

    ends = jnp.where(first, grad_entry, final)
    ends_mine = ends[:own_rows]
    ends_other = swap_half(ends[own_rows:].astype(bf16)).astype(f32)
    ends_out = jnp.stack(
        [
            jnp.where(half == 0, ends_mine, ends_other),
            jnp.where(half == 0, ends_other, ends_mine),
        ]
    )[None, :, None]

    joined_b_grad, up_b_grad = halves
    joined_b_grad = joined_b_grad.reshape(3, 2, pair)
    up_b_grad = up_b_grad.reshape(2, hidden_units)
    shared = jnp.stack(
        [jnp.where(first, gain_first, gain_last), jnp.where(first, bias_first, bias_last), *shared]
    )
    shared = butterfly(shared, "tensor", 2).reshape(-1)
    thin_size = 2 * pair + hidden_units
    thin_rows = -(-(8 * width + thin_size) // (16 * width)) * 16

    def last_task(at, fence):
        line = [shared, joined_b_grad[0, at], joined_b_grad[2, at], up_b_grad[at]]
        line.append(jnp.zeros((thin_rows * width - 8 * width - thin_size,), f32))
        line = jnp.concatenate(line).astype(bf16)
        return jnp.concatenate(last_parts(at, fence) + [line.reshape(thin_rows, width)])

    sums.tasks.append(last_task)
    sums.step(ends, shared, joined_b_grad)
    summed = [part.astype(f32) for part in sums.finish()]
    thin_grad = summed[-1][-thin_rows:].reshape(-1)
    shared = thin_grad[: 8 * width].reshape(8, width)
    thin_grad = thin_grad[8 * width : 8 * width + thin_size]
    middle_at = len(summed) // 2 - 1
    down_grad = jnp.concatenate(summed[:middle_at])
    up_grad = jnp.concatenate(
        [part.reshape(-1, hidden_units) for part in summed[middle_at:-2]]
    )
    rest = jnp.concatenate([summed[-2], summed[-1][:-thin_rows]]).reshape(4, heads * HD, width)
    out_grad = rest[0]
    joined_grad = rest[1:].reshape(3, heads, HD, width).transpose(3, 1, 0, 2).reshape(width, -1)

    gain_grads = jnp.stack([shared[0], shared[2], shared[4]])[None]
    bias_grads = jnp.stack([shared[1], shared[3], shared[5]])[None]
    return (
        ends_out,
        embed_stat,
        gain_grads,
        bias_grads,
        joined_grad[None],
        thin_grad[: 2 * pair].reshape(1, 2, pair),
        out_grad[None],
        shared[6][None],
        up_grad[None],
        thin_grad[2 * pair :][None],
        down_grad[None],
        shared[7][None],
    )


def solution(mesh):
    return jax.shard_map(
        local,
        mesh=mesh,
        in_specs=(
            P("section", None, "dp", "tensor", None),
            P(None, "dp", None),
            P("section", None, None),
            P("section", None, None),
            P("section", None, "tensor"),
            P("section", None, "tensor"),
            P("section", "tensor", None),
            P("section", None),
            P("section", None, "tensor"),
            P("section", "tensor"),
            P("section", "tensor", None),
            P("section", None),
        ),
        out_specs=(
            P("section", None, "dp", "tensor", None),
            P(),
            P("section", None, None),
            P("section", None, None),
            P("section", None, "tensor"),
            P("section", None, "tensor"),
            P("section", "tensor", None),
            P("section", None),
            P("section", None, "tensor"),
            P("section", "tensor"),
            P("section", "tensor", None),
            P("section", None),
        ),
        check_vma=False,
    )
```

```python
from functools import partial

import jax
import jax.numpy as jnp
from jax import lax
from jax.experimental import pallas as pl
from jax.experimental.pallas import tpu as pltpu
from jax.sharding import PartitionSpec as P

H = 16
HD = 64
eps = 1e-05

f32 = jnp.float32
bf16 = jnp.bfloat16

MIB = 1024 * 1024


def swap_half(array):
    size = lax.axis_size("tensor")
    pairs = [(i, (i + size // 2) % size) for i in range(size)]
    return lax.ppermute(array, "tensor", pairs)


def from_rank(array, by):
    size = lax.axis_size("tensor")
    ranks = size // 2
    pairs = [
        (m * ranks + (j + by) % ranks, m * ranks + j) for m in range(2) for j in range(ranks)
    ]
    return lax.ppermute(array, "tensor", pairs)


def from_section(array, by):
    size = lax.axis_size("section")
    pairs = [(i, i + by) for i in range(size) if 0 <= i + by < size]
    return lax.ppermute(array, "section", pairs)


def gather_rows(own):
    ranks = lax.axis_size("tensor") // 2
    return [own] + [from_rank(own, k) for k in range(1, ranks)]


def scatter_sum(part_of):
    ranks = lax.axis_size("tensor") // 2
    arrived = [from_rank(part_of(k).astype(bf16), ranks - k) for k in range(1, ranks)]
    own = lax.optimization_barrier(part_of(0))
    return own + sum(part.astype(f32) for part in arrived)


def butterfly(array, axis, parts=1):
    size = lax.axis_size(axis)
    step = 1
    while step < size // parts:
        array = array + lax.ppermute(array, axis, [(i, i ^ step) for i in range(size)])
        step *= 2
    return array


def from_all(share, axis):
    size = lax.axis_size(axis)
    shares = [share]
    for by in range(1, size):
        shares.append(lax.ppermute(share, axis, [(i, (i + by) % size) for i in range(size)]))
    return shares


def after(array, *others):
    return lax.optimization_barrier((array, *others))[0]


def total(*parts):
    return sum(part.astype(f32) for part in parts)


class RowSums:
    ends = [(0, 1), (1, 0), (2, 3), (3, 2)]
    centre = [(1, 2), (2, 1)]

    def __init__(self, axis):
        self.axis = axis
        self.line = lax.axis_size(axis) == 4
        place = lax.axis_index(axis)
        self.outer = (place == 0) | (place == 3)
        self.tasks, self.owns, self.pars = [], [], []
        self.swapped, self.partials, self.sent = [], [], []
        self.from_end, self.from_centre = [], []

    def part(self, done, at, others):
        if len(done) < len(self.tasks):
            fence = (lambda array: after(array, *others)) if others else lambda array: array
            part = self.tasks[len(done)](at, fence).astype(bf16)
            done.append(lax.optimization_barrier(part))

    def own(self, *others):
        self.part(self.owns, 0, others)

    def par(self, *others):
        self.part(self.pars, 1, others)

    def swap(self, *others):
        part = self.pars[len(self.swapped)]
        self.swapped.append(swap_half(after(part, *others) if others else part))

    def step(self, *others, prepare=True):
        step, count = len(self.sent), len(self.tasks)
        come = self.swapped[step : step + 1] + self.from_end[-1:] + self.from_centre[-1:]
        come += list(others)
        fresh = total(self.owns[step], self.swapped[step]) if step < count else None
        if not self.line:
            self.sent.append(fresh.astype(bf16))
            come = self.swapped[step : step + 1]
        else:
            done = total(self.partials[step - 2], self.from_centre[step - 2]) if step >= 2 else fresh
            if fresh is None:
                fresh = done
            done = jnp.pad(done, ((0, fresh.shape[0] - done.shape[0]), (0, 0)))
            to_end = jnp.where(self.outer, fresh, done).astype(bf16)
            self.sent.append(after(to_end, *come))
            self.from_end.append(lax.ppermute(self.sent[-1], self.axis, self.ends))
            if 0 <= step - 1 < count:
                parts = (self.owns[step - 1], self.swapped[step - 1], self.from_end[step - 1])
                self.partials.append(total(*parts).astype(bf16))
                middle = after(self.partials[-1], *come)
                self.from_centre.append(lax.ppermute(middle, self.axis, self.centre))
        while len(self.swapped) < min(step + 3, len(self.pars)):
            self.swap(*come)
        if prepare:
            made = self.sent[-1:] + self.partials[-1:]
            self.own(*made)
            self.par(*made)
        return come

    def finish(self):
        count = len(self.tasks)
        while len(self.sent) < count + (2 if self.line else 0):
            self.step()
        if not self.line:
            return [lax.psum(chunk, self.axis) for chunk in self.sent]
        sums = [
            jnp.where(self.outer, self.from_end[n + 2], self.sent[n + 2]) for n in range(count)
        ]
        return [part[: self.owns[n].shape[0]] for n, part in enumerate(sums)]


def dot(left, right):
    return jnp.dot(left, right, preferred_element_type=f32)


def dot_nt(left, right):
    return lax.dot_general(left, right, (((1,), (1,)), ((), ())), preferred_element_type=f32)


def dot_tn(left, right):
    return lax.dot_general(left, right, (((0,), (0,)), ((), ())), preferred_element_type=f32)


def normalise(values_in):
    centre = jnp.mean(values_in, axis=-1, keepdims=True)
    centred = values_in - centre
    variance = jnp.mean(centred * centred, axis=-1, keepdims=True)
    scale = lax.rsqrt(variance + eps)
    return centred * scale, scale


def layer_norm(values_in, gain, bias):
    return normalise(values_in)[0] * gain + bias


def layer_norm_back(values_in, gain, grad):
    hat, scale = normalise(values_in)
    scaled = grad * gain
    inner = jnp.mean(scaled, axis=-1, keepdims=True)
    along = jnp.mean(scaled * hat, axis=-1, keepdims=True)
    grad_in = scale * (scaled - inner - hat * along)
    return grad_in, jnp.sum(grad * hat, axis=0), jnp.sum(grad, axis=0)


def variance_total(values_in):
    centred = values_in - jnp.mean(values_in, axis=-1, keepdims=True)
    return jnp.sum(jnp.mean(centred * centred, axis=-1))


def gelu_pair(pre):
    root = 0.7978845608028654
    square = pre * pre
    bent = jnp.tanh(root * pre * (1.0 + 0.044715 * square))
    rise = 0.5 * (1.0 + bent)
    slope = rise + 0.5 * pre * (1.0 - bent * bent) * root * (1.0 + 3 * 0.044715 * square)
    return pre * rise, slope


def fetch(scratch, pieces, blocks_ref, rows, scale=None):
    slots = pieces[0].shape[0] // rows
    for b in range(len(pieces) * slots):
        part = pieces[b // slots][pl.ds((b % slots) * rows, rows), :]
        if scale is not None:
            part = part * scale
        scratch[pl.ds(pl.multiple_of(blocks_ref[b] * rows, rows), rows), :] = part


def only_head(values, e):
    lane = lax.broadcasted_iota(jnp.int32, values.shape, 1)
    return jnp.where((lane >= HD) == (e == 1), values, jnp.zeros_like(values))


def fill_distance(far, seg_col_ref, seg_row_ref, rows, flipped):
    length = far.shape[0]
    for one in range(length // rows):
        for two in range(one + 1):
            low, high = pl.ds(one * rows, rows), pl.ds(two * rows, rows)
            if flipped:
                low, high = high, low
            shape = (rows, rows)
            along = lax.broadcasted_iota(jnp.int32, shape, 0) - lax.broadcasted_iota(
                jnp.int32, shape, 1
            )
            gap = (-along if flipped else along) + (one - two) * rows
            same = seg_col_ref[low, :] == seg_row_ref[:, high]
            far[low, high] = jnp.where(same & (gap >= 0), gap.astype(f32), 1e32)


def attend_kernel(count, rows, blocks_ref, slopes_ref, seg_col_ref, seg_row_ref, *refs):
    q_in, k_in, v_in = refs[:count], refs[count : 2 * count], refs[2 * count : 3 * count]
    context_out = refs[3 * count : 4 * count]
    log_out = refs[4 * count]
    queries, keys, values, context, far = refs[4 * count + 1 :]
    pair = pl.program_id(0)
    length = queries.shape[0]

    @pl.when(pair == 0)
    def _():
        fill_distance(far, seg_col_ref, seg_row_ref, rows, False)

    fetch(queries, q_in, blocks_ref, rows, jnp.asarray(HD**-0.5, bf16))
    fetch(keys, k_in, blocks_ref, rows)
    fetch(values, v_in, blocks_ref, rows)
    lane = lax.broadcasted_iota(jnp.int32, (rows, 128), 1)
    for i in range(length // rows):
        here, until = pl.ds(i * rows, rows), pl.ds(0, (i + 1) * rows)
        total = None
        logs = None
        for e in range(2):
            slope = slopes_ref[2 * pair + e]
            scores = dot_nt(only_head(queries[here, :], e), keys[until, :])
            scores = scores - slope * far[here, until]
            highest = jnp.max(scores, axis=1, keepdims=True)
            shifted = jnp.exp(scores - highest)
            summed = jnp.sum(shifted, axis=1, keepdims=True)
            part = dot(shifted.astype(bf16), only_head(values[until, :], e)) / summed
            log = highest + jnp.log(summed)
            total = part if e == 0 else total + part
            logs = jnp.broadcast_to(log, (rows, 128)) if e == 0 else jnp.where(lane == 1, log, logs)
        context[here, :] = total.astype(bf16)
        log_out[0, :, here] = logs.T[:8]
    slots = q_in[0].shape[0] // rows
    for b in range(count * slots):
        context_out[b // slots][pl.ds((b % slots) * rows, rows), :] = context[
            pl.ds(pl.multiple_of(blocks_ref[b] * rows, rows), rows), :
        ]


def attend_back_kernel(count, rows, blocks_ref, slopes_ref, seg_col_ref, seg_row_ref, *refs):
    q_in, k_in, v_in, c_in, g_in = [refs[n * count : (n + 1) * count] for n in range(5)]
    log_in = refs[5 * count]
    grad_out = refs[5 * count + 1 : 6 * count + 1]
    queries, keys, values, context, grads, far, grad_q, grad_k, grad_v = refs[6 * count + 1 :]
    pair = pl.program_id(0)
    length = queries.shape[0]
    width = grad_out[0].shape[1] // 3

    @pl.when(pair == 0)
    def _():
        fill_distance(far, seg_col_ref, seg_row_ref, rows, True)

    fetch(queries, q_in, blocks_ref, rows, jnp.asarray(HD**-0.5, bf16))
    fetch(keys, k_in, blocks_ref, rows)
    fetch(values, v_in, blocks_ref, rows)
    fetch(context, c_in, blocks_ref, rows)
    fetch(grads, g_in, blocks_ref, rows)
    head_of = lax.broadcasted_iota(jnp.int32, (8, 128), 1) // HD
    chosen = (head_of == lax.broadcasted_iota(jnp.int32, (8, 128), 0)).astype(f32)
    inner = lax.dot_general(
        chosen,
        context[...].astype(f32) * grads[...].astype(f32),
        (((1,), (1,)), ((), ())),
        precision=lax.Precision.HIGHEST,
        preferred_element_type=f32,
    )
    grad_k[...] = jnp.zeros_like(grad_k)
    grad_v[...] = jnp.zeros_like(grad_v)
    for i in range(length // rows):
        here, until = pl.ds(i * rows, rows), pl.ds(0, (i + 1) * rows)
        chances, slants, heads_q, heads_g, heads_k = [], [], [], [], []
        for e in range(2):
            slope = slopes_ref[2 * pair + e]
            query = only_head(queries[here, :], e)
            grad = only_head(grads[here, :], e)
            scores = dot_nt(keys[until, :], query)
            scores = scores - slope * far[until, here] - log_in[0, e : e + 1, here]
            chance = jnp.exp(scores)
            grad_chance = dot_nt(values[until, :], grad)
            slant = chance * (grad_chance - inner[e : e + 1, i * rows : (i + 1) * rows])
            chances.append(chance.astype(bf16))
            slants.append(slant.astype(bf16))
            heads_q.append(query)
            heads_g.append(grad)
            heads_k.append(only_head(keys[until, :], e))
        grad_v[until, :] += dot(jnp.concatenate(chances, axis=1), jnp.concatenate(heads_g, axis=0))
        grad_k[until, :] += dot(jnp.concatenate(slants, axis=1), jnp.concatenate(heads_q, axis=0))
        grad_q[here, :] = (
            dot_tn(slants[0], heads_k[0]) + dot_tn(slants[1], heads_k[1])
        ) * HD**-0.5
    slots = q_in[0].shape[0] // rows
    for b in range(count * slots):
        place = pl.ds(pl.multiple_of(blocks_ref[b] * rows, rows), rows)
        for n, part in enumerate((grad_q, grad_k, grad_v)):
            column = pl.ds(pl.multiple_of(n * width + pair * 128, 128), 128)
            grad_out[b // slots][pl.ds((b % slots) * rows, rows), column] = part[place, :].astype(
                bf16
            )


def attention_specs(joined, segment_ids):
    count, rows_of_piece = len(joined), joined[0].shape[0]
    pairs = joined[0].shape[1] // (3 * 128)
    length = segment_ids.shape[0]
    smem = pl.BlockSpec(memory_space=pltpu.SMEM)
    common = [
        smem,
        smem,
        pl.BlockSpec((length, 1), lambda p: (0, 0)),
        pl.BlockSpec((1, length), lambda p: (0, 0)),
    ]

    def column(n):
        return pl.BlockSpec((rows_of_piece, 128), lambda p: (0, n * pairs + p))

    log_spec = pl.BlockSpec((1, 8, length), lambda p: (p, 0, 0))
    return count, rows_of_piece, pairs, length, common, column, log_spec


def attend(joined, order, segment_ids, slopes):
    count, piece, pairs, length, common, column, log_spec = attention_specs(joined, segment_ids)
    rows = length // order.shape[0]
    low = pltpu.VMEM((length, 128), bf16)
    out = pl.pallas_call(
        partial(attend_kernel, count, rows),
        grid=(pairs,),
        in_specs=common + [column(n) for n in range(3) for _ in range(count)],
        out_specs=[column(0)] * count + [log_spec],
        out_shape=[jax.ShapeDtypeStruct((piece, pairs * 128), bf16)] * count
        + [jax.ShapeDtypeStruct((pairs, 8, length), f32)],
        scratch_shapes=[low, low, low, low, pltpu.VMEM((length, length), f32)],
        compiler_params=pltpu.CompilerParams(vmem_limit_bytes=14 * MIB),
        cost_estimate=pl.CostEstimate(
            flops=pairs * 128 * length,
            bytes_accessed=length * pairs * 128,
            transcendentals=0,
        ),
        name="attend",
    )(order, slopes, segment_ids[:, None], segment_ids[None], *joined, *joined, *joined)
    return out[:count], out[count]


def attend_back(joined, context, logs, grad_context, order, segment_ids, slopes):
    count, piece, pairs, length, common, column, log_spec = attention_specs(joined, segment_ids)
    rows = length // order.shape[0]
    low, high = pltpu.VMEM((length, 128), bf16), pltpu.VMEM((length, 128), f32)
    whole = pl.BlockSpec((piece, 3 * pairs * 128), lambda p: (0, 0))
    out = pl.pallas_call(
        partial(attend_back_kernel, count, rows),
        grid=(pairs,),
        in_specs=common
        + [column(n) for n in range(3) for _ in range(count)]
        + [column(0)] * (2 * count)
        + [log_spec],
        out_specs=[whole] * count,
        out_shape=[jax.ShapeDtypeStruct((piece, 3 * pairs * 128), bf16)] * count,
        scratch_shapes=[low] * 5 + [pltpu.VMEM((length, length), f32)] + [high] * 3,
        compiler_params=pltpu.CompilerParams(vmem_limit_bytes=24 * MIB),
        cost_estimate=pl.CostEstimate(
            flops=pairs * 128 * length,
            bytes_accessed=length * pairs * 128,
            transcendentals=0,
        ),
        name="attend_back",
    )(
        order,
        slopes,
        segment_ids[:, None],
        segment_ids[None],
        *joined,
        *joined,
        *joined,
        *context,
        *grad_context,
        logs,
    )
    return out


def head_group(normed, group, places, segment_ids):
    joined_w, joined_b, out_w, slopes = group
    joined = [(dot(part, joined_w) + joined_b).astype(bf16) for part in normed]
    context, log_total = attend(joined, places, segment_ids, slopes)
    return joined, context, log_total, out_w


def forward(hidden, weights, normed, parts):
    _, _, gain_two, bias_two, _, _, _, out_b, up_w, up_b, down_w, down_b = weights
    middle = (
        hidden
        + scatter_sum(lambda k: sum(dot(part[1][k], part[3]) for part in parts))
        + out_b
    )
    spread = gather_rows(layer_norm(middle, gain_two, bias_two).astype(bf16))
    active, bent = [], []
    for part in spread:
        act, slope = gelu_pair(dot(part, up_w) + up_b)
        act, slope = lax.optimization_barrier((act.astype(bf16), slope.astype(bf16)))
        active.append(act)
        bent.append(slope)
    result = middle + scatter_sum(lambda k: dot(active[k], down_w)) + down_b
    kept = (hidden, normed, *parts[0][:3], middle, spread, active, bent)
    return result, kept


def backward(grad, kept, weights, places, segment_ids, slopes, sums=None, wholes=None):
    hidden, normed, joined, context, log_total, middle, spread, active, bent = kept
    gain_one, bias_one, gain_two, bias_two, joined_w, joined_b, out_w, out_b = weights[:8]
    up_w, up_b, down_w, down_b = weights[8:]
    count = len(normed)

    grad_down_b = jnp.sum(grad, axis=0)
    grads = gather_rows(grad.astype(bf16))
    rows, units, width = out_w.shape[0] // 2, down_w.shape[0] // 2, out_w.shape[1]
    tasks = sums.tasks if sums else []
    whole_normed, whole_context, whole_spread, whole_active = wholes or [None] * 4
    whole_grads = jnp.concatenate(grads)
    for c in range(0, units, 2 * rows):
        tasks.append(
            lambda at, fence, c=c: dot_tn(
                whole_active[:, at * units + c : at * units + c + 2 * rows], fence(whole_grads)
            )
        )
    if sums:
        sums.par()
        sums.swap()
        grads[0] = after(grads[0], sums.pars[0])
        sums.own()
        sums.par()
    grad_pre = [
        lax.optimization_barrier(
            (dot_nt(grads[k], down_w) * bent[k].astype(f32)).astype(bf16)
        )
        for k in range(count)
    ]
    up_b_grad = sum(jnp.sum(part, axis=0, dtype=f32) for part in grad_pre)
    whole_pre = jnp.concatenate(grad_pre)
    high = 2 * rows * width // units
    for c in range(0, width, high):
        tasks.append(
            lambda at, fence, c=c: dot_tn(
                fence(whole_spread)[:, c : c + high], whole_pre[:, at * units : (at + 1) * units]
            ).reshape(2 * rows, width)
        )
    grad_spread = scatter_sum(lambda k: dot_nt(grad_pre[k], up_w))
    grad_two, gain_two_grad, bias_two_grad = layer_norm_back(middle, gain_two, grad_spread)
    grad_middle = grad + grad_two
    out_b_grad = jnp.sum(grad_middle, axis=0)
    grads = gather_rows(grad_middle.astype(bf16))
    if sums:
        sums.own()
        sums.par()
        sums.par()
        sums.step(prepare=False)
        grads[0] = after(grads[0], sums.sent[0], sums.owns[1], sums.pars[3])
    grad_context = [dot_nt(part, out_w).astype(bf16) for part in grads]
    grad_joined = attend_back(
        joined, context, log_total, grad_context, places, segment_ids, slopes
    )
    whole_middle, whole_joined = jnp.concatenate(grads), jnp.concatenate(grad_joined)

    def of_joined(n, at, fence):
        first = (2 * n + at) * rows
        return dot_tn(whole_joined[:, first : first + rows], fence(whole_normed)).astype(bf16)

    def of_out(at, fence):
        left = whole_context[:, at * rows : (at + 1) * rows]
        return dot_tn(left, fence(whole_middle)).astype(bf16)

    tasks.append(
        lambda at, fence: jnp.concatenate([of_out(at, fence), of_joined(0, at, fence)])
    )
    last_parts = lambda at, fence: [of_joined(1, at, fence), of_joined(2, at, fence)]
    if sums:
        come = sums.step(grad_joined[0])
        grad_joined = [after(part, *come) for part in grad_joined]
    joined_b_grad = sum(jnp.sum(part, axis=0, dtype=f32) for part in grad_joined)
    grad_normed = scatter_sum(lambda k: dot_nt(grad_joined[k], joined_w))
    grad_one, gain_one_grad, bias_one_grad = layer_norm_back(hidden, gain_one, grad_normed)
    halves = (joined_b_grad, up_b_grad)
    shared = (
        gain_one_grad,
        bias_one_grad,
        gain_two_grad,
        bias_two_grad,
        out_b_grad,
        grad_down_b,
    )
    return grad_middle + grad_one, last_parts, halves, shared


def local(
    boundary,
    segments,
    gains,
    biases,
    qkv_weight,
    qv_bias,
    out_weight,
    out_bias,
    up_weight,
    up_bias,
    down_weight,
    down_bias,
):
    first = lax.axis_index("section") == 0
    tensor = lax.axis_size("tensor")
    ranks = tensor // 2
    place = lax.axis_index("tensor")
    half, rank = place // ranks, place % ranks
    micro_count, own_rows, width = boundary.shape[1], boundary.shape[3], boundary.shape[4]
    heads = qkv_weight.shape[2] // (3 * HD)
    hidden_units = up_weight.shape[2]

    rows = boundary[0, :, 0]
    mine = jnp.where(half == 0, rows[0], rows[1])
    other = jnp.where(half == 0, rows[1], rows[0])

    order = [(rank + k) % ranks for k in range(ranks)]
    blocks = [b for r in order for b in (half * ranks + r, (1 - half) * ranks + r)]
    places = jnp.stack(blocks)
    segment_ids = jnp.where(half == 0, segments[0, 0], segments[1, 0])
    partner = (1 - half) * ranks + rank
    head_index = jnp.concatenate(
        [p * heads + lax.iota(jnp.int32, heads) for p in (place, partner)]
    )
    slopes = jnp.exp2(-8.0 * (head_index + 1).astype(f32) / H)

    def share(array, row=0):
        part = (array.shape[1] - row) // lax.axis_size("dp")
        at = row + lax.axis_index("dp") * part
        return lax.dynamic_slice(array, (0, at, 0), (1, part, array.shape[2]))[0]

    def arrange(joined):
        return joined.reshape(-1, heads, 3, HD).transpose(0, 2, 1, 3).reshape(joined.shape)

    up_rows, down_rows = width // 2, hidden_units // 2
    own_share = arrange(share(qkv_weight))
    joined_share = swap_half(own_share)
    thin = jnp.concatenate([qv_bias[0].reshape(-1), up_bias[0]])
    pair = qv_bias.shape[2]
    pieces, rest = [], thin
    for _ in range(3):
        pieces.append(lax.reduce_precision(rest, 8, 7))
        rest = rest - pieces[-1]
    pieces = jnp.concatenate(pieces).astype(bf16)
    thin_lines = -(-pieces.size // (16 * width)) * 16
    pieces = jnp.pad(pieces, (0, thin_lines * width - pieces.size)).reshape(thin_lines, width)
    mixed = swap_half(after(jnp.concatenate([other, out_weight[0], pieces]), own_share))
    other_end, other_out = mixed[:own_rows], mixed[own_rows:-thin_lines]
    pieces = mixed[-thin_lines:].reshape(-1)[: 3 * thin.size].reshape(3, -1).astype(f32)
    thin_other = pieces[0] + pieces[1] + pieces[2]
    up_piece, down_piece = share(up_weight, up_rows), share(down_weight, down_rows)
    up_lines = up_piece.size // width
    mixed_share = swap_half(
        after(jnp.concatenate([up_piece.reshape(-1, width), down_piece]), own_share)
    )
    up_direct = up_weight[0, :up_rows].reshape(-1, width)
    direct = swap_half(
        after(jnp.concatenate([up_direct, down_weight[0, :down_rows]]), joined_share)
    )
    other_up = direct[: up_direct.shape[0]].reshape(up_rows, hidden_units)
    other_down = direct[up_direct.shape[0] :]
    own_joined = arrange(qkv_weight[0])

    def passed_round(shares, whole, row, column):
        for step, part in enumerate(shares):
            at = (lax.axis_index("dp") - step) % len(shares)
            whole = lax.dynamic_update_slice(whole, part, (row + at * part.shape[0], column))
        return whole

    none = jnp.zeros((), bf16)
    joined_shares = from_all(joined_share, "dp")
    mixed_shares = from_all(after(mixed_share, *joined_shares[1:]), "dp")
    other_joined = passed_round(joined_shares, jnp.zeros_like(own_joined), 0, 0)
    other_joined = lax.optimization_barrier(other_joined)
    own_end = jnp.concatenate([mine, after(other_end, joined_share)]).astype(f32)
    nothing = jnp.zeros((pair,), f32)
    own_b = jnp.concatenate([thin[:pair], nothing, thin[pair : 2 * pair]])
    other_b = jnp.concatenate([thin_other[:pair], nothing, thin_other[pair : 2 * pair]])
    joined_b = jnp.concatenate([own_b.reshape(3, -1), other_b.reshape(3, -1)], axis=1).reshape(-1)
    up_b = jnp.concatenate([thin[2 * pair :], thin_other[2 * pair :]])
    weights = (gains[0, 1], biases[0, 1], gains[0, 2], biases[0, 2])

    spread_total = variance_total(after(rows, joined_share).astype(f32))
    spread_total = jnp.where(first, spread_total, 0.0)
    token_count = micro_count * own_rows * tensor * lax.axis_size("dp")
    stat = butterfly(jnp.broadcast_to(spread_total, (1, 128)), "section")
    own_b = after(own_b, stat)
    start = layer_norm(own_end, gains[0, 0], biases[0, 0])
    normed = gather_rows(layer_norm(start, weights[0], weights[1]).astype(bf16))
    own_group = (own_joined, own_b, out_weight[0], slopes[:heads])
    own_part = head_group(normed, own_group, places, segment_ids)
    other_b = after(other_b, own_part[1][0])
    other_group = (other_joined, other_b, other_out, slopes[heads:])
    other_part = head_group(normed, other_group, places, segment_ids)

    up_shares = [part[:up_lines].reshape(-1, hidden_units) for part in mixed_shares]
    down_shares = [part[up_lines:] for part in mixed_shares]
    up_w = jnp.pad(other_up, ((0, width - up_rows), (0, 0)))
    up_w = jnp.concatenate([up_weight[0], passed_round(up_shares, up_w, up_rows, 0)], axis=1)
    down_w = jnp.concatenate([down_weight[0], other_down])
    down_w = jnp.pad(down_w, ((0, hidden_units - down_rows), (0, 0)))
    down_w = passed_round(down_shares, down_w, hidden_units + down_rows, 0)
    joined_w = jnp.concatenate(
        [own_joined.reshape(width, 3, -1), other_joined.reshape(width, 3, -1)], axis=2
    ).reshape(width, -1)
    out_w = jnp.concatenate([out_weight[0], other_out], axis=0)
    joined_w, out_w, up_w, down_w = [
        lax.optimization_barrier(part) for part in (joined_w, out_w, up_w, down_w)
    ]
    weights += (joined_w, joined_b, out_w, out_bias[0], up_w, up_b, down_w, down_bias[0])
    result, _ = forward(start, weights, normed, (own_part, other_part))
    stat = after(stat, result)
    for axis in ("tensor", "dp"):
        stat = butterfly(stat, axis)
    embed_stat = stat[0, 0] / token_count
    passed = after(from_section(result.astype(bf16), 1), stat, joined_w, out_w).astype(f32)
    hidden = jnp.where(first, start, passed)
    normed = gather_rows(layer_norm(hidden, weights[0], weights[1]).astype(bf16))
    whole_part = head_group(normed, (joined_w, joined_b, out_w, slopes), places, segment_ids)
    result, kept = forward(hidden, weights, normed, (whole_part,))
    final = layer_norm(result, gains[0, 0], biases[0, 0])

    grad_last, gain_last, bias_last = layer_norm_back(result, gains[0, 0], own_end)
    grad_passed = backward(grad_last, kept, weights, places, segment_ids, slopes)[0]
    normed, context, spread, active = kept[1], kept[3], kept[6], kept[7]
    wholes = [jnp.concatenate(parts) for parts in (normed, context, spread, active)]
    arrived = after(from_section(grad_passed.astype(bf16), -1), *wholes).astype(f32)
    grad = jnp.where(first, arrived, grad_last)
    sums = RowSums("dp")
    grad_start, last_parts, halves, shared = backward(
        grad, kept, weights, places, segment_ids, slopes, sums, wholes
    )
    grad_entry, gain_first, bias_first = layer_norm_back(own_end, gains[0, 0], grad_start)

    ends = jnp.where(first, grad_entry, final)
    ends_mine = ends[:own_rows]
    ends_other = ends[own_rows:].astype(bf16)
    joined_b_grad, up_b_grad = halves
    joined_b_grad = joined_b_grad.reshape(3, 2, pair)
    up_b_grad = up_b_grad.reshape(2, hidden_units)
    shared = jnp.stack(
        [jnp.where(first, gain_first, gain_last), jnp.where(first, bias_first, bias_last), *shared]
    )
    shared = butterfly(shared, "tensor", 2).reshape(-1)
    thin_size = 2 * pair + hidden_units
    thin_rows = -(-(8 * width + thin_size) // (16 * width)) * 16

    def last_task(at, fence):
        line = [shared, joined_b_grad[0, at], joined_b_grad[2, at], up_b_grad[at]]
        line.append(jnp.zeros((thin_rows * width - 8 * width - thin_size,), f32))
        line = jnp.concatenate(line).astype(bf16)
        return jnp.concatenate(last_parts(at, fence) + [line.reshape(thin_rows, width)])

    sums.step()
    sums.tasks.append(last_task)
    sums.step(grad_start)
    sums.step(ends, shared, joined_b_grad)
    while len(sums.swapped) < len(sums.tasks):
        sums.step()
    ends_other = swap_half(after(ends_other, sums.sent[-1])).astype(f32)
    ends_out = jnp.stack(
        [
            jnp.where(half == 0, ends_mine, ends_other),
            jnp.where(half == 0, ends_other, ends_mine),
        ]
    )[None, :, None]
    summed = [part.astype(f32) for part in sums.finish()]
    thin_grad = summed[-1][-thin_rows:].reshape(-1)
    shared = thin_grad[: 8 * width].reshape(8, width)
    thin_grad = thin_grad[8 * width : 8 * width + thin_size]
    middle_at = len(summed) // 2 - 1
    down_grad = jnp.concatenate(summed[:middle_at])
    up_grad = jnp.concatenate(
        [part.reshape(-1, hidden_units) for part in summed[middle_at:-2]]
    )
    rest = jnp.concatenate([summed[-2], summed[-1][:-thin_rows]]).reshape(4, heads * HD, width)
    out_grad = rest[0]
    joined_grad = rest[1:].reshape(3, heads, HD, width).transpose(3, 1, 0, 2).reshape(width, -1)

    gain_grads = jnp.stack([shared[0], shared[2], shared[4]])[None]
    bias_grads = jnp.stack([shared[1], shared[3], shared[5]])[None]
    return (
        ends_out,
        embed_stat,
        gain_grads,
        bias_grads,
        joined_grad[None],
        thin_grad[: 2 * pair].reshape(1, 2, pair),
        out_grad[None],
        shared[6][None],
        up_grad[None],
        thin_grad[2 * pair :][None],
        down_grad[None],
        shared[7][None],
    )


def solution(mesh):
    return jax.shard_map(
        local,
        mesh=mesh,
        in_specs=(
            P("section", None, "dp", "tensor", None),
            P(None, "dp", None),
            P("section", None, None),
            P("section", None, None),
            P("section", None, "tensor"),
            P("section", None, "tensor"),
            P("section", "tensor", None),
            P("section", None),
            P("section", None, "tensor"),
            P("section", "tensor"),
            P("section", "tensor", None),
            P("section", None),
        ),
        out_specs=(
            P("section", None, "dp", "tensor", None),
            P(),
            P("section", None, None),
            P("section", None, None),
            P("section", None, "tensor"),
            P("section", None, "tensor"),
            P("section", "tensor", None),
            P("section", None),
            P("section", None, "tensor"),
            P("section", "tensor"),
            P("section", "tensor", None),
            P("section", None),
        ),
        check_vma=False,
    )
```

```python
from functools import partial

import jax
import jax.numpy as jnp
from jax import lax
from jax.experimental import pallas as pl
from jax.experimental.pallas import tpu as pltpu
from jax.sharding import PartitionSpec as P

H = 16
HD = 64
eps = 1e-05

f32 = jnp.float32
bf16 = jnp.bfloat16

MIB = 1024 * 1024


def swap_half(array):
    size = lax.axis_size("tensor")
    pairs = [(i, (i + size // 2) % size) for i in range(size)]
    return lax.ppermute(array, "tensor", pairs)


def from_rank(array, by):
    size = lax.axis_size("tensor")
    ranks = size // 2
    pairs = [
        (m * ranks + (j + by) % ranks, m * ranks + j) for m in range(2) for j in range(ranks)
    ]
    return lax.ppermute(array, "tensor", pairs)


def from_section(array, by):
    size = lax.axis_size("section")
    pairs = [(i, i + by) for i in range(size) if 0 <= i + by < size]
    return lax.ppermute(array, "section", pairs)


def gather_rows(own):
    ranks = lax.axis_size("tensor") // 2
    return [own] + [from_rank(own, k) for k in range(1, ranks)]


def scatter_sum(part_of):
    ranks = lax.axis_size("tensor") // 2
    arrived = [from_rank(part_of(k).astype(bf16), ranks - k) for k in range(1, ranks)]
    own = lax.optimization_barrier(part_of(0))
    return own + sum(part.astype(f32) for part in arrived)


def butterfly(array, axis, parts=1):
    size = lax.axis_size(axis)
    step = 1
    while step < size // parts:
        array = array + lax.ppermute(array, axis, [(i, i ^ step) for i in range(size)])
        step *= 2
    return array


def from_all(share, axis):
    size = lax.axis_size(axis)
    shares = [share]
    for by in range(1, size):
        shares.append(lax.ppermute(share, axis, [(i, (i + by) % size) for i in range(size)]))
    return shares


def after(array, *others):
    return lax.optimization_barrier((array, *others))[0]


def total(*parts):
    return sum(part.astype(f32) for part in parts)


class RowSums:
    ends = [(0, 1), (1, 0), (2, 3), (3, 2)]
    centre = [(1, 2), (2, 1)]

    def __init__(self, axis):
        self.axis = axis
        self.line = lax.axis_size(axis) == 4
        place = lax.axis_index(axis)
        self.outer = (place == 0) | (place == 3)
        self.tasks, self.owns, self.pars = [], [], []
        self.swapped, self.partials, self.sent = [], [], []
        self.from_end, self.from_centre = [], []

    def part(self, done, at, others):
        if len(done) < len(self.tasks):
            fence = (lambda array: after(array, *others)) if others else lambda array: array
            part = self.tasks[len(done)](at, fence).astype(bf16)
            done.append(lax.optimization_barrier(part))

    def own(self, *others):
        self.part(self.owns, 0, others)

    def par(self, *others):
        self.part(self.pars, 1, others)

    def swap(self, *others):
        part = self.pars[len(self.swapped)]
        self.swapped.append(swap_half(after(part, *others) if others else part))

    def step(self, *others, prepare=True):
        step, count = len(self.sent), len(self.tasks)
        come = self.swapped[step : step + 1] + self.from_end[-1:] + self.from_centre[-1:]
        come += list(others)
        fresh = total(self.owns[step], self.swapped[step]) if step < count else None
        if not self.line:
            self.sent.append(fresh.astype(bf16))
            come = self.swapped[step : step + 1]
        else:
            done = total(self.partials[step - 2], self.from_centre[step - 2]) if step >= 2 else fresh
            if fresh is None:
                fresh = done
            done = jnp.pad(done, ((0, fresh.shape[0] - done.shape[0]), (0, 0)))
            to_end = jnp.where(self.outer, fresh, done).astype(bf16)
            self.sent.append(after(to_end, *come))
            self.from_end.append(lax.ppermute(self.sent[-1], self.axis, self.ends))
            if 0 <= step - 1 < count:
                parts = (self.owns[step - 1], self.swapped[step - 1], self.from_end[step - 1])
                self.partials.append(total(*parts).astype(bf16))
                middle = after(self.partials[-1], *come)
                self.from_centre.append(lax.ppermute(middle, self.axis, self.centre))
        while len(self.swapped) < min(step + 3, len(self.pars)):
            self.swap(*come)
        made = self.sent[-1:] + self.partials[-1:]
        if prepare:
            self.own(*made)
            self.par(*made)
        return made

    def finish(self):
        count = len(self.tasks)
        while len(self.sent) < count + (2 if self.line else 0):
            self.step()
        if not self.line:
            return [lax.psum(chunk, self.axis) for chunk in self.sent]
        sums = [
            jnp.where(self.outer, self.from_end[n + 2], self.sent[n + 2]) for n in range(count)
        ]
        return [part[: self.owns[n].shape[0]] for n, part in enumerate(sums)]


def dot(left, right):
    return jnp.dot(left, right, preferred_element_type=f32)


def dot_nt(left, right):
    return lax.dot_general(left, right, (((1,), (1,)), ((), ())), preferred_element_type=f32)


def dot_tn(left, right):
    return lax.dot_general(left, right, (((0,), (0,)), ((), ())), preferred_element_type=f32)


def normalise(values_in):
    centre = jnp.mean(values_in, axis=-1, keepdims=True)
    centred = values_in - centre
    variance = jnp.mean(centred * centred, axis=-1, keepdims=True)
    scale = lax.rsqrt(variance + eps)
    return centred * scale, scale


def layer_norm(values_in, gain, bias):
    return normalise(values_in)[0] * gain + bias


def layer_norm_back(values_in, gain, grad):
    hat, scale = normalise(values_in)
    scaled = grad * gain
    inner = jnp.mean(scaled, axis=-1, keepdims=True)
    along = jnp.mean(scaled * hat, axis=-1, keepdims=True)
    grad_in = scale * (scaled - inner - hat * along)
    return grad_in, jnp.sum(grad * hat, axis=0), jnp.sum(grad, axis=0)


def variance_total(values_in):
    centred = values_in - jnp.mean(values_in, axis=-1, keepdims=True)
    return jnp.sum(jnp.mean(centred * centred, axis=-1))


def gelu_pair(pre):
    root = 0.7978845608028654
    square = pre * pre
    bent = jnp.tanh(root * pre * (1.0 + 0.044715 * square))
    rise = 0.5 * (1.0 + bent)
    slope = rise + 0.5 * pre * (1.0 - bent * bent) * root * (1.0 + 3 * 0.044715 * square)
    return pre * rise, slope


def fetch(scratch, pieces, blocks_ref, rows, scale=None):
    slots = pieces[0].shape[0] // rows
    for b in range(len(pieces) * slots):
        part = pieces[b // slots][pl.ds((b % slots) * rows, rows), :]
        if scale is not None:
            part = part * scale
        scratch[pl.ds(pl.multiple_of(blocks_ref[b] * rows, rows), rows), :] = part


def only_head(values, e):
    lane = lax.broadcasted_iota(jnp.int32, values.shape, 1)
    return jnp.where((lane >= HD) == (e == 1), values, jnp.zeros_like(values))


def fill_distance(far, seg_col_ref, seg_row_ref, rows, flipped):
    length = far.shape[0]
    for one in range(length // rows):
        for two in range(one + 1):
            low, high = pl.ds(one * rows, rows), pl.ds(two * rows, rows)
            if flipped:
                low, high = high, low
            shape = (rows, rows)
            along = lax.broadcasted_iota(jnp.int32, shape, 0) - lax.broadcasted_iota(
                jnp.int32, shape, 1
            )
            gap = (-along if flipped else along) + (one - two) * rows
            same = seg_col_ref[low, :] == seg_row_ref[:, high]
            far[low, high] = jnp.where(same & (gap >= 0), gap.astype(f32), 1e32)


def attend_kernel(count, rows, blocks_ref, slopes_ref, seg_col_ref, seg_row_ref, *refs):
    q_in, k_in, v_in = refs[:count], refs[count : 2 * count], refs[2 * count : 3 * count]
    context_out = refs[3 * count : 4 * count]
    log_out = refs[4 * count]
    queries, keys, values, context, far = refs[4 * count + 1 :]
    pair = pl.program_id(0)
    length = queries.shape[0]

    @pl.when(pair == 0)
    def _():
        fill_distance(far, seg_col_ref, seg_row_ref, rows, False)

    fetch(queries, q_in, blocks_ref, rows, jnp.asarray(HD**-0.5, bf16))
    fetch(keys, k_in, blocks_ref, rows)
    fetch(values, v_in, blocks_ref, rows)
    lane = lax.broadcasted_iota(jnp.int32, (rows, 128), 1)
    for i in range(length // rows):
        here, until = pl.ds(i * rows, rows), pl.ds(0, (i + 1) * rows)
        total = None
        logs = None
        for e in range(2):
            slope = slopes_ref[2 * pair + e]
            scores = dot_nt(only_head(queries[here, :], e), keys[until, :])
            scores = scores - slope * far[here, until]
            highest = jnp.max(scores, axis=1, keepdims=True)
            shifted = jnp.exp(scores - highest)
            summed = jnp.sum(shifted, axis=1, keepdims=True)
            part = dot(shifted.astype(bf16), only_head(values[until, :], e)) / summed
            log = highest + jnp.log(summed)
            total = part if e == 0 else total + part
            logs = jnp.broadcast_to(log, (rows, 128)) if e == 0 else jnp.where(lane == 1, log, logs)
        context[here, :] = total.astype(bf16)
        log_out[0, :, here] = logs.T[:8]
    slots = q_in[0].shape[0] // rows
    for b in range(count * slots):
        context_out[b // slots][pl.ds((b % slots) * rows, rows), :] = context[
            pl.ds(pl.multiple_of(blocks_ref[b] * rows, rows), rows), :
        ]


def attend_back_kernel(count, rows, blocks_ref, slopes_ref, seg_col_ref, seg_row_ref, *refs):
    q_in, k_in, v_in, c_in, g_in = [refs[n * count : (n + 1) * count] for n in range(5)]
    log_in = refs[5 * count]
    grad_out = refs[5 * count + 1 : 6 * count + 1]
    queries, keys, values, context, grads, far, grad_q, grad_k, grad_v = refs[6 * count + 1 :]
    pair = pl.program_id(0)
    length = queries.shape[0]
    width = grad_out[0].shape[1] // 3

    @pl.when(pair == 0)
    def _():
        fill_distance(far, seg_col_ref, seg_row_ref, rows, True)

    fetch(queries, q_in, blocks_ref, rows, jnp.asarray(HD**-0.5, bf16))
    fetch(keys, k_in, blocks_ref, rows)
    fetch(values, v_in, blocks_ref, rows)
    fetch(context, c_in, blocks_ref, rows)
    fetch(grads, g_in, blocks_ref, rows)
    head_of = lax.broadcasted_iota(jnp.int32, (8, 128), 1) // HD
    chosen = (head_of == lax.broadcasted_iota(jnp.int32, (8, 128), 0)).astype(f32)
    inner = lax.dot_general(
        chosen,
        context[...].astype(f32) * grads[...].astype(f32),
        (((1,), (1,)), ((), ())),
        precision=lax.Precision.HIGHEST,
        preferred_element_type=f32,
    )
    grad_k[...] = jnp.zeros_like(grad_k)
    grad_v[...] = jnp.zeros_like(grad_v)
    for i in range(length // rows):
        here, until = pl.ds(i * rows, rows), pl.ds(0, (i + 1) * rows)
        chances, slants, heads_q, heads_g, heads_k = [], [], [], [], []
        for e in range(2):
            slope = slopes_ref[2 * pair + e]
            query = only_head(queries[here, :], e)
            grad = only_head(grads[here, :], e)
            scores = dot_nt(keys[until, :], query)
            scores = scores - slope * far[until, here] - log_in[0, e : e + 1, here]
            chance = jnp.exp(scores)
            grad_chance = dot_nt(values[until, :], grad)
            slant = chance * (grad_chance - inner[e : e + 1, i * rows : (i + 1) * rows])
            chances.append(chance.astype(bf16))
            slants.append(slant.astype(bf16))
            heads_q.append(query)
            heads_g.append(grad)
            heads_k.append(only_head(keys[until, :], e))
        grad_v[until, :] += dot(jnp.concatenate(chances, axis=1), jnp.concatenate(heads_g, axis=0))
        grad_k[until, :] += dot(jnp.concatenate(slants, axis=1), jnp.concatenate(heads_q, axis=0))
        grad_q[here, :] = (
            dot_tn(slants[0], heads_k[0]) + dot_tn(slants[1], heads_k[1])
        ) * HD**-0.5
    slots = q_in[0].shape[0] // rows
    for b in range(count * slots):
        place = pl.ds(pl.multiple_of(blocks_ref[b] * rows, rows), rows)
        for n, part in enumerate((grad_q, grad_k, grad_v)):
            column = pl.ds(pl.multiple_of(n * width + pair * 128, 128), 128)
            grad_out[b // slots][pl.ds((b % slots) * rows, rows), column] = part[place, :].astype(
                bf16
            )


def attention_specs(joined, segment_ids):
    count, rows_of_piece = len(joined), joined[0].shape[0]
    pairs = joined[0].shape[1] // (3 * 128)
    length = segment_ids.shape[0]
    smem = pl.BlockSpec(memory_space=pltpu.SMEM)
    common = [
        smem,
        smem,
        pl.BlockSpec((length, 1), lambda p: (0, 0)),
        pl.BlockSpec((1, length), lambda p: (0, 0)),
    ]

    def column(n):
        return pl.BlockSpec((rows_of_piece, 128), lambda p: (0, n * pairs + p))

    log_spec = pl.BlockSpec((1, 8, length), lambda p: (p, 0, 0))
    return count, rows_of_piece, pairs, length, common, column, log_spec


def attend(joined, order, segment_ids, slopes):
    count, piece, pairs, length, common, column, log_spec = attention_specs(joined, segment_ids)
    rows = length // order.shape[0]
    low = pltpu.VMEM((length, 128), bf16)
    out = pl.pallas_call(
        partial(attend_kernel, count, rows),
        grid=(pairs,),
        in_specs=common + [column(n) for n in range(3) for _ in range(count)],
        out_specs=[column(0)] * count + [log_spec],
        out_shape=[jax.ShapeDtypeStruct((piece, pairs * 128), bf16)] * count
        + [jax.ShapeDtypeStruct((pairs, 8, length), f32)],
        scratch_shapes=[low, low, low, low, pltpu.VMEM((length, length), f32)],
        compiler_params=pltpu.CompilerParams(vmem_limit_bytes=14 * MIB),
        cost_estimate=pl.CostEstimate(
            flops=pairs * 128 * length,
            bytes_accessed=length * pairs * 128,
            transcendentals=0,
        ),
        name="attend",
    )(order, slopes, segment_ids[:, None], segment_ids[None], *joined, *joined, *joined)
    return out[:count], out[count]


def attend_back(joined, context, logs, grad_context, order, segment_ids, slopes):
    count, piece, pairs, length, common, column, log_spec = attention_specs(joined, segment_ids)
    rows = length // order.shape[0]
    low, high = pltpu.VMEM((length, 128), bf16), pltpu.VMEM((length, 128), f32)
    whole = pl.BlockSpec((piece, 3 * pairs * 128), lambda p: (0, 0))
    out = pl.pallas_call(
        partial(attend_back_kernel, count, rows),
        grid=(pairs,),
        in_specs=common
        + [column(n) for n in range(3) for _ in range(count)]
        + [column(0)] * (2 * count)
        + [log_spec],
        out_specs=[whole] * count,
        out_shape=[jax.ShapeDtypeStruct((piece, 3 * pairs * 128), bf16)] * count,
        scratch_shapes=[low] * 5 + [pltpu.VMEM((length, length), f32)] + [high] * 3,
        compiler_params=pltpu.CompilerParams(vmem_limit_bytes=18 * MIB),
        cost_estimate=pl.CostEstimate(
            flops=pairs * 128 * length,
            bytes_accessed=length * pairs * 128,
            transcendentals=0,
        ),
        name="attend_back",
    )(
        order,
        slopes,
        segment_ids[:, None],
        segment_ids[None],
        *joined,
        *joined,
        *joined,
        *context,
        *grad_context,
        logs,
    )
    return out


def head_group(normed, group, places, segment_ids):
    joined_w, joined_b, out_w, slopes = group
    joined = [(dot(part, joined_w) + joined_b).astype(bf16) for part in normed]
    context, log_total = attend(joined, places, segment_ids, slopes)
    return joined, context, log_total, out_w


def forward(hidden, weights, normed, parts):
    _, _, gain_two, bias_two, _, _, _, out_b, up_w, up_b, down_w, down_b = weights
    middle = (
        hidden
        + scatter_sum(lambda k: sum(dot(part[1][k], part[3]) for part in parts))
        + out_b
    )
    spread = gather_rows(layer_norm(middle, gain_two, bias_two).astype(bf16))
    active, bent = [], []
    for part in spread:
        act, slope = gelu_pair(dot(part, up_w) + up_b)
        act, slope = lax.optimization_barrier((act.astype(bf16), slope.astype(bf16)))
        active.append(act)
        bent.append(slope)
    result = middle + scatter_sum(lambda k: dot(active[k], down_w)) + down_b
    kept = (hidden, normed, *parts[0][:3], middle, spread, active, bent)
    return result, kept


def backward(grad, kept, weights, places, segment_ids, slopes, sums=None, wholes=None):
    hidden, normed, joined, context, log_total, middle, spread, active, bent = kept
    gain_one, bias_one, gain_two, bias_two, joined_w, joined_b, out_w, out_b = weights[:8]
    up_w, up_b, down_w, down_b = weights[8:]
    count = len(normed)

    grad_down_b = jnp.sum(grad, axis=0)
    grads = gather_rows(grad.astype(bf16))
    rows, units, width = out_w.shape[0] // 2, down_w.shape[0] // 2, out_w.shape[1]
    tasks = sums.tasks if sums else []
    whole_normed, whole_context, whole_spread, whole_active = wholes or [None] * 4
    whole_grads = jnp.concatenate(grads)
    for c in range(0, units, 2 * rows):
        tasks.append(
            lambda at, fence, c=c: dot(
                whole_active[at * units + c : at * units + c + 2 * rows], fence(whole_grads)
            )
        )
    if sums:
        sums.par()
        sums.swap()
        grads[0] = after(grads[0], sums.pars[0])
        sums.own()
        sums.par()
    grad_pre = [
        lax.optimization_barrier(
            (dot_nt(grads[k], down_w) * bent[k].astype(f32)).astype(bf16)
        )
        for k in range(count)
    ]
    up_b_grad = sum(jnp.sum(part, axis=0, dtype=f32) for part in grad_pre)
    whole_pre = jnp.concatenate(grad_pre)
    high = 2 * rows * width // units
    for c in range(0, width, high):
        tasks.append(
            lambda at, fence, c=c: dot(
                fence(whole_spread)[c : c + high], whole_pre[:, at * units : (at + 1) * units]
            ).reshape(2 * rows, width)
        )
    grad_spread = scatter_sum(lambda k: dot_nt(grad_pre[k], up_w))
    grad_two, gain_two_grad, bias_two_grad = layer_norm_back(middle, gain_two, grad_spread)
    grad_middle = grad + grad_two
    out_b_grad = jnp.sum(grad_middle, axis=0)
    grads = gather_rows(grad_middle.astype(bf16))
    if sums:
        sums.own()
        sums.par()
        sums.par()
        sums.step(prepare=False)
        grads[0] = after(grads[0], sums.sent[0], sums.owns[1], sums.pars[3])
    grad_context = [dot_nt(part, out_w).astype(bf16) for part in grads]
    grad_joined = attend_back(
        joined, context, log_total, grad_context, places, segment_ids, slopes
    )
    whole_middle, whole_joined = jnp.concatenate(grads), jnp.concatenate(grad_joined)

    def of_joined(n, at, fence):
        first = (2 * n + at) * rows
        return dot_tn(whole_joined[:, first : first + rows], fence(whole_normed)).astype(bf16)

    def of_out(at, fence):
        left = whole_context[at * rows : (at + 1) * rows]
        return dot(left, fence(whole_middle)).astype(bf16)

    tasks.append(
        lambda at, fence: jnp.concatenate([of_out(at, fence), of_joined(0, at, fence)])
    )
    last_parts = lambda at, fence: [of_joined(1, at, fence), of_joined(2, at, fence)]
    if sums:
        made = sums.step(grad_joined[0]) + sums.from_centre[:1]
        grad_joined = [after(part, *made) for part in grad_joined]
    joined_b_grad = sum(jnp.sum(part, axis=0, dtype=f32) for part in grad_joined)
    grad_normed = scatter_sum(lambda k: dot_nt(grad_joined[k], joined_w))
    if sums:
        sums.step()
        grad_normed = after(grad_normed, *sums.from_centre[1:])
    grad_one, gain_one_grad, bias_one_grad = layer_norm_back(hidden, gain_one, grad_normed)
    halves = (joined_b_grad, up_b_grad)
    shared = (
        gain_one_grad,
        bias_one_grad,
        gain_two_grad,
        bias_two_grad,
        out_b_grad,
        grad_down_b,
    )
    return grad_middle + grad_one, last_parts, halves, shared


def local(
    boundary,
    segments,
    gains,
    biases,
    qkv_weight,
    qv_bias,
    out_weight,
    out_bias,
    up_weight,
    up_bias,
    down_weight,
    down_bias,
):
    first = lax.axis_index("section") == 0
    tensor = lax.axis_size("tensor")
    ranks = tensor // 2
    place = lax.axis_index("tensor")
    half, rank = place // ranks, place % ranks
    micro_count, own_rows, width = boundary.shape[1], boundary.shape[3], boundary.shape[4]
    heads = qkv_weight.shape[2] // (3 * HD)
    hidden_units = up_weight.shape[2]

    rows = boundary[0, :, 0]
    mine = jnp.where(half == 0, rows[0], rows[1])
    other = jnp.where(half == 0, rows[1], rows[0])

    order = [(rank + k) % ranks for k in range(ranks)]
    blocks = [b for r in order for b in (half * ranks + r, (1 - half) * ranks + r)]
    places = jnp.stack(blocks)
    segment_ids = jnp.where(half == 0, segments[0, 0], segments[1, 0])
    partner = (1 - half) * ranks + rank
    head_index = jnp.concatenate(
        [p * heads + lax.iota(jnp.int32, heads) for p in (place, partner)]
    )
    slopes = jnp.exp2(-8.0 * (head_index + 1).astype(f32) / H)

    def share(array, row=0):
        part = (array.shape[1] - row) // lax.axis_size("dp")
        at = row + lax.axis_index("dp") * part
        return lax.dynamic_slice(array, (0, at, 0), (1, part, array.shape[2]))[0]

    def arrange(joined):
        return joined.reshape(-1, heads, 3, HD).transpose(0, 2, 1, 3).reshape(joined.shape)

    up_rows, down_rows = width // 2, hidden_units // 2
    own_share = arrange(share(qkv_weight))
    joined_share = swap_half(own_share)
    thin = jnp.concatenate([qv_bias[0].reshape(-1), up_bias[0]])
    pair = qv_bias.shape[2]
    pieces, rest = [], thin
    for _ in range(3):
        pieces.append(lax.reduce_precision(rest, 8, 7))
        rest = rest - pieces[-1]
    pieces = jnp.concatenate(pieces).astype(bf16)
    thin_lines = -(-pieces.size // (16 * width)) * 16
    pieces = jnp.pad(pieces, (0, thin_lines * width - pieces.size)).reshape(thin_lines, width)
    mixed = swap_half(after(jnp.concatenate([other, out_weight[0], pieces]), own_share))
    other_end, other_out = mixed[:own_rows], mixed[own_rows:-thin_lines]
    pieces = mixed[-thin_lines:].reshape(-1)[: 3 * thin.size].reshape(3, -1).astype(f32)
    thin_other = pieces[0] + pieces[1] + pieces[2]
    up_piece, down_piece = share(up_weight, up_rows), share(down_weight, down_rows)
    up_lines = up_piece.size // width
    mixed_share = swap_half(
        after(jnp.concatenate([up_piece.reshape(-1, width), down_piece]), own_share)
    )
    up_direct = up_weight[0, :up_rows].reshape(-1, width)
    direct = swap_half(
        after(jnp.concatenate([up_direct, down_weight[0, :down_rows]]), joined_share)
    )
    other_up = direct[: up_direct.shape[0]].reshape(up_rows, hidden_units)
    other_down = direct[up_direct.shape[0] :]
    own_joined = arrange(qkv_weight[0])

    def passed_round(shares, whole, row, column):
        for step, part in enumerate(shares):
            at = (lax.axis_index("dp") - step) % len(shares)
            whole = lax.dynamic_update_slice(whole, part, (row + at * part.shape[0], column))
        return whole

    none = jnp.zeros((), bf16)
    joined_shares = from_all(joined_share, "dp")
    mixed_shares = from_all(after(mixed_share, *joined_shares[1:]), "dp")
    other_joined = passed_round(joined_shares, jnp.zeros_like(own_joined), 0, 0)
    other_joined = lax.optimization_barrier(other_joined)
    own_end = jnp.concatenate([mine, after(other_end, joined_share)]).astype(f32)
    nothing = jnp.zeros((pair,), f32)
    own_b = jnp.concatenate([thin[:pair], nothing, thin[pair : 2 * pair]])
    other_b = jnp.concatenate([thin_other[:pair], nothing, thin_other[pair : 2 * pair]])
    joined_b = jnp.concatenate([own_b.reshape(3, -1), other_b.reshape(3, -1)], axis=1).reshape(-1)
    up_b = jnp.concatenate([thin[2 * pair :], thin_other[2 * pair :]])
    weights = (gains[0, 1], biases[0, 1], gains[0, 2], biases[0, 2])

    spread_total = variance_total(after(rows, joined_share).astype(f32))
    spread_total = jnp.where(first, spread_total, 0.0)
    token_count = micro_count * own_rows * tensor * lax.axis_size("dp")
    stat = butterfly(jnp.broadcast_to(spread_total, (1, 128)), "section")
    own_b = after(own_b, stat)
    start = layer_norm(own_end, gains[0, 0], biases[0, 0])
    normed = gather_rows(layer_norm(start, weights[0], weights[1]).astype(bf16))
    own_group = (own_joined, own_b, out_weight[0], slopes[:heads])
    own_part = head_group(normed, own_group, places, segment_ids)
    other_b = after(other_b, own_part[1][0])
    other_group = (other_joined, other_b, other_out, slopes[heads:])
    other_part = head_group(normed, other_group, places, segment_ids)

    up_shares = [part[:up_lines].reshape(-1, hidden_units) for part in mixed_shares]
    down_shares = [part[up_lines:] for part in mixed_shares]
    up_w = jnp.pad(other_up, ((0, width - up_rows), (0, 0)))
    up_w = jnp.concatenate([up_weight[0], passed_round(up_shares, up_w, up_rows, 0)], axis=1)
    down_w = jnp.concatenate([down_weight[0], other_down])
    down_w = jnp.pad(down_w, ((0, hidden_units - down_rows), (0, 0)))
    down_w = passed_round(down_shares, down_w, hidden_units + down_rows, 0)
    joined_w = jnp.concatenate(
        [own_joined.reshape(width, 3, -1), other_joined.reshape(width, 3, -1)], axis=2
    ).reshape(width, -1)
    out_w = jnp.concatenate([out_weight[0], other_out], axis=0)
    joined_w, out_w, up_w, down_w = [
        lax.optimization_barrier(part) for part in (joined_w, out_w, up_w, down_w)
    ]
    weights += (joined_w, joined_b, out_w, out_bias[0], up_w, up_b, down_w, down_bias[0])
    result, _ = forward(start, weights, normed, (own_part, other_part))
    stat = after(stat, result)
    for axis in ("tensor", "dp"):
        stat = butterfly(stat, axis)
    embed_stat = stat[0, 0] / token_count
    passed = after(from_section(result.astype(bf16), 1), stat, joined_w, out_w).astype(f32)
    hidden = jnp.where(first, start, passed)
    normed = gather_rows(layer_norm(hidden, weights[0], weights[1]).astype(bf16))
    whole_part = head_group(normed, (joined_w, joined_b, out_w, slopes), places, segment_ids)
    result, kept = forward(hidden, weights, normed, (whole_part,))
    final = layer_norm(result, gains[0, 0], biases[0, 0])

    grad_last, gain_last, bias_last = layer_norm_back(result, gains[0, 0], own_end)
    grad_passed = backward(grad_last, kept, weights, places, segment_ids, slopes)[0]
    normed, context, spread, active = kept[1], kept[3], kept[6], kept[7]
    wholes = [jnp.concatenate(normed)] + [
        jnp.concatenate([part.T for part in parts], axis=1) for parts in (context, spread, active)
    ]
    arrived = after(from_section(grad_passed.astype(bf16), -1), *wholes).astype(f32)
    grad = jnp.where(first, arrived, grad_last)
    sums = RowSums("dp")
    grad_start, last_parts, halves, shared = backward(
        grad, kept, weights, places, segment_ids, slopes, sums, wholes
    )
    grad_entry, gain_first, bias_first = layer_norm_back(own_end, gains[0, 0], grad_start)

    ends = jnp.where(first, grad_entry, final)
    ends_mine = ends[:own_rows]
    ends_other = ends[own_rows:].astype(bf16)
    joined_b_grad, up_b_grad = halves
    joined_b_grad = joined_b_grad.reshape(3, 2, pair)
    up_b_grad = up_b_grad.reshape(2, hidden_units)
    shared = jnp.stack(
        [jnp.where(first, gain_first, gain_last), jnp.where(first, bias_first, bias_last), *shared]
    )
    shared = butterfly(shared, "tensor", 2).reshape(-1)
    thin_size = 2 * pair + hidden_units
    thin_rows = -(-(8 * width + thin_size) // (16 * width)) * 16

    def last_task(at, fence):
        line = [shared, joined_b_grad[0, at], joined_b_grad[2, at], up_b_grad[at]]
        line.append(jnp.zeros((thin_rows * width - 8 * width - thin_size,), f32))
        line = jnp.concatenate(line).astype(bf16)
        return jnp.concatenate(last_parts(at, fence) + [line.reshape(thin_rows, width)])

    sums.tasks.append(last_task)
    sums.step()
    sums.step(ends, shared, joined_b_grad)
    while len(sums.swapped) < len(sums.tasks):
        sums.step()
    ends_other = swap_half(after(ends_other, sums.sent[-1])).astype(f32)
    ends_out = jnp.stack(
        [
            jnp.where(half == 0, ends_mine, ends_other),
            jnp.where(half == 0, ends_other, ends_mine),
        ]
    )[None, :, None]
    summed = [part.astype(f32) for part in sums.finish()]
    thin_grad = summed[-1][-thin_rows:].reshape(-1)
    shared = thin_grad[: 8 * width].reshape(8, width)
    thin_grad = thin_grad[8 * width : 8 * width + thin_size]
    middle_at = len(summed) // 2 - 1
    down_grad = jnp.concatenate(summed[:middle_at])
    up_grad = jnp.concatenate(
        [part.reshape(-1, hidden_units) for part in summed[middle_at:-2]]
    )
    rest = jnp.concatenate([summed[-2], summed[-1][:-thin_rows]]).reshape(4, heads * HD, width)
    out_grad = rest[0]
    joined_grad = rest[1:].reshape(3, heads, HD, width).transpose(3, 1, 0, 2).reshape(width, -1)

    gain_grads = jnp.stack([shared[0], shared[2], shared[4]])[None]
    bias_grads = jnp.stack([shared[1], shared[3], shared[5]])[None]
    return (
        ends_out,
        embed_stat,
        gain_grads,
        bias_grads,
        joined_grad[None],
        thin_grad[: 2 * pair].reshape(1, 2, pair),
        out_grad[None],
        shared[6][None],
        up_grad[None],
        thin_grad[2 * pair :][None],
        down_grad[None],
        shared[7][None],
    )


def solution(mesh):
    return jax.shard_map(
        local,
        mesh=mesh,
        in_specs=(
            P("section", None, "dp", "tensor", None),
            P(None, "dp", None),
            P("section", None, None),
            P("section", None, None),
            P("section", None, "tensor"),
            P("section", None, "tensor"),
            P("section", "tensor", None),
            P("section", None),
            P("section", None, "tensor"),
            P("section", "tensor"),
            P("section", "tensor", None),
            P("section", None),
        ),
        out_specs=(
            P("section", None, "dp", "tensor", None),
            P(),
            P("section", None, None),
            P("section", None, None),
            P("section", None, "tensor"),
            P("section", None, "tensor"),
            P("section", "tensor", None),
            P("section", None),
            P("section", None, "tensor"),
            P("section", "tensor"),
            P("section", "tensor", None),
            P("section", None),
        ),
        check_vma=False,
    )
```

```python
from functools import partial

import jax
import jax.numpy as jnp
from jax import lax
from jax.experimental import pallas as pl
from jax.experimental.pallas import tpu as pltpu
from jax.sharding import PartitionSpec as P

H = 16
HD = 64
eps = 1e-05

f32 = jnp.float32
bf16 = jnp.bfloat16

MIB = 1024 * 1024


def swap_half(array):
    size = lax.axis_size("tensor")
    pairs = [(i, (i + size // 2) % size) for i in range(size)]
    return lax.ppermute(array, "tensor", pairs)


def from_rank(array, by):
    size = lax.axis_size("tensor")
    ranks = size // 2
    pairs = [
        (m * ranks + (j + by) % ranks, m * ranks + j) for m in range(2) for j in range(ranks)
    ]
    return lax.ppermute(array, "tensor", pairs)


def from_section(array, by):
    size = lax.axis_size("section")
    pairs = [(i, i + by) for i in range(size) if 0 <= i + by < size]
    return lax.ppermute(array, "section", pairs)


def gather_rows(own):
    ranks = lax.axis_size("tensor") // 2
    return [own] + [from_rank(own, k) for k in range(1, ranks)]


def scatter_sum(part_of):
    ranks = lax.axis_size("tensor") // 2
    arrived = [from_rank(part_of(k).astype(bf16), ranks - k) for k in range(1, ranks)]
    own = lax.optimization_barrier(part_of(0))
    return own + sum(part.astype(f32) for part in arrived)


def butterfly(array, axis, parts=1):
    size = lax.axis_size(axis)
    step = 1
    while step < size // parts:
        array = array + lax.ppermute(array, axis, [(i, i ^ step) for i in range(size)])
        step *= 2
    return array


def from_all(share, axis):
    size = lax.axis_size(axis)
    shares = [share]
    for by in range(1, size):
        shares.append(lax.ppermute(share, axis, [(i, (i + by) % size) for i in range(size)]))
    return shares


def after(array, *others):
    return lax.optimization_barrier((array, *others))[0]


def total(*parts):
    return sum(part.astype(f32) for part in parts)


class RowSums:
    ends = [(0, 1), (1, 0), (2, 3), (3, 2)]
    centre = [(1, 2), (2, 1)]

    def __init__(self, axis):
        self.axis = axis
        self.line = lax.axis_size(axis) == 4
        place = lax.axis_index(axis)
        self.outer = (place == 0) | (place == 3)
        self.tasks, self.owns, self.pars = [], [], []
        self.swapped, self.partials, self.sent = [], [], []
        self.from_end, self.from_centre = [], []

    def part(self, done, at, others):
        if len(done) < len(self.tasks):
            fence = (lambda array: after(array, *others)) if others else lambda array: array
            part = self.tasks[len(done)](at, fence).astype(bf16)
            done.append(lax.optimization_barrier(part))

    def own(self, *others):
        self.part(self.owns, 0, others)

    def par(self, *others):
        self.part(self.pars, 1, others)

    def swap(self, *others):
        part = self.pars[len(self.swapped)]
        self.swapped.append(swap_half(after(part, *others) if others else part))

    def step(self, *others, prepare=True):
        step, count = len(self.sent), len(self.tasks)
        come = self.swapped[step : step + 1] + self.from_end[-1:] + self.from_centre[-1:]
        come += list(others)
        fresh = total(self.owns[step], self.swapped[step]) if step < count else None
        if not self.line:
            self.sent.append(fresh.astype(bf16))
            come = self.swapped[step : step + 1]
        else:
            done = total(self.partials[step - 2], self.from_centre[step - 2]) if step >= 2 else fresh
            if fresh is None:
                fresh = done
            done = jnp.pad(done, ((0, fresh.shape[0] - done.shape[0]), (0, 0)))
            to_end = jnp.where(self.outer, fresh, done).astype(bf16)
            self.sent.append(after(to_end, *come))
            self.from_end.append(lax.ppermute(self.sent[-1], self.axis, self.ends))
            if 0 <= step - 1 < count:
                parts = (self.owns[step - 1], self.swapped[step - 1], self.from_end[step - 1])
                self.partials.append(total(*parts).astype(bf16))
                middle = after(self.partials[-1], *come)
                self.from_centre.append(lax.ppermute(middle, self.axis, self.centre))
        while len(self.swapped) < min(step + 3, len(self.pars)):
            self.swap(*come)
        made = self.sent[-1:] + self.partials[-1:]
        if prepare:
            self.own(*made)
            self.par(*made)
        return made

    def finish(self):
        count = len(self.tasks)
        while len(self.sent) < count + (2 if self.line else 0):
            self.step()
        if not self.line:
            return [lax.psum(chunk, self.axis) for chunk in self.sent]
        sums = [
            jnp.where(self.outer, self.from_end[n + 2], self.sent[n + 2]) for n in range(count)
        ]
        return [part[: self.owns[n].shape[0]] for n, part in enumerate(sums)]


def dot(left, right):
    return jnp.dot(left, right, preferred_element_type=f32)


def dot_nt(left, right):
    return lax.dot_general(left, right, (((1,), (1,)), ((), ())), preferred_element_type=f32)


def dot_tn(left, right):
    return lax.dot_general(left, right, (((0,), (0,)), ((), ())), preferred_element_type=f32)


def normalise(values_in):
    centre = jnp.mean(values_in, axis=-1, keepdims=True)
    centred = values_in - centre
    variance = jnp.mean(centred * centred, axis=-1, keepdims=True)
    scale = lax.rsqrt(variance + eps)
    return centred * scale, scale


def layer_norm(values_in, gain, bias):
    return normalise(values_in)[0] * gain + bias


def layer_norm_back(values_in, gain, grad):
    hat, scale = normalise(values_in)
    scaled = grad * gain
    inner = jnp.mean(scaled, axis=-1, keepdims=True)
    along = jnp.mean(scaled * hat, axis=-1, keepdims=True)
    grad_in = scale * (scaled - inner - hat * along)
    return grad_in, jnp.sum(grad * hat, axis=0), jnp.sum(grad, axis=0)


def variance_total(values_in):
    centred = values_in - jnp.mean(values_in, axis=-1, keepdims=True)
    return jnp.sum(jnp.mean(centred * centred, axis=-1))


def gelu_pair(pre):
    root = 0.7978845608028654
    square = pre * pre
    bent = jnp.tanh(pre * (root + root * 0.044715 * square))
    rise = 0.5 + 0.5 * bent
    slope = rise * (1.0 + pre * (1.0 - bent) * (root + 3 * root * 0.044715 * square))
    return pre * rise, slope


def fetch(scratch, pieces, blocks_ref, rows, scale=None):
    slots = pieces[0].shape[0] // rows
    for b in range(len(pieces) * slots):
        part = pieces[b // slots][pl.ds((b % slots) * rows, rows), :]
        if scale is not None:
            part = part * scale
        scratch[pl.ds(pl.multiple_of(blocks_ref[b] * rows, rows), rows), :] = part


def only_head(values, e):
    lane = lax.broadcasted_iota(jnp.int32, values.shape, 1)
    return jnp.where((lane >= HD) == (e == 1), values, jnp.zeros_like(values))


def fill_distance(far, seg_col_ref, seg_row_ref, rows, flipped, span=1):
    length = far.shape[0]
    for one in range(length // rows):
        for two in range(one // span * span + span):
            low, high = pl.ds(one * rows, rows), pl.ds(two * rows, rows)
            if flipped:
                low, high = high, low
            shape = (rows, rows)
            along = lax.broadcasted_iota(jnp.int32, shape, 0) - lax.broadcasted_iota(
                jnp.int32, shape, 1
            )
            gap = (-along if flipped else along) + (one - two) * rows
            same = seg_col_ref[low, :] == seg_row_ref[:, high]
            far[low, high] = jnp.where(same & (gap >= 0), gap.astype(f32), 1e32)


def attend_kernel(count, rows, blocks_ref, slopes_ref, seg_col_ref, seg_row_ref, *refs):
    q_in, k_in, v_in = refs[:count], refs[count : 2 * count], refs[2 * count : 3 * count]
    context_out = refs[3 * count : 4 * count]
    log_out = refs[4 * count]
    queries, keys, values, context, far = refs[4 * count + 1 :]
    pair = pl.program_id(0)
    length = queries.shape[0]

    @pl.when(pair == 0)
    def _():
        fill_distance(far, seg_col_ref, seg_row_ref, rows, False, 2)

    fetch(queries, q_in, blocks_ref, rows, jnp.asarray(HD**-0.5, bf16))
    fetch(keys, k_in, blocks_ref, rows)
    fetch(values, v_in, blocks_ref, rows)
    many = 2 * rows
    lane = lax.broadcasted_iota(jnp.int32, (many, 128), 1)
    for i in range(length // many):
        here, until = pl.ds(i * many, many), pl.ds(0, (i + 1) * many)
        total = None
        logs = None
        for e in range(2):
            slope = slopes_ref[2 * pair + e]
            scores = dot_nt(only_head(queries[here, :], e), keys[until, :])
            scores = scores - slope * far[here, until]
            highest = jnp.max(scores, axis=1, keepdims=True)
            shifted = jnp.exp(scores - highest)
            summed = jnp.sum(shifted, axis=1, keepdims=True)
            part = dot(shifted.astype(bf16), only_head(values[until, :], e)) / summed
            log = highest + jnp.log(summed)
            total = part if e == 0 else total + part
            logs = jnp.broadcast_to(log, (many, 128)) if e == 0 else jnp.where(lane == 1, log, logs)
        context[here, :] = total.astype(bf16)
        log_out[0, :, here] = logs.T[:8]
    slots = q_in[0].shape[0] // rows
    for b in range(count * slots):
        context_out[b // slots][pl.ds((b % slots) * rows, rows), :] = context[
            pl.ds(pl.multiple_of(blocks_ref[b] * rows, rows), rows), :
        ]


def attend_back_kernel(count, rows, blocks_ref, slopes_ref, seg_col_ref, seg_row_ref, *refs):
    q_in, k_in, v_in, c_in, g_in = [refs[n * count : (n + 1) * count] for n in range(5)]
    log_in = refs[5 * count]
    grad_out = refs[5 * count + 1 : 6 * count + 1]
    queries, keys, values, context, grads, far, grad_q, grad_k, grad_v = refs[6 * count + 1 :]
    pair = pl.program_id(0)
    length = queries.shape[0]
    width = grad_out[0].shape[1] // 3

    @pl.when(pair == 0)
    def _():
        fill_distance(far, seg_col_ref, seg_row_ref, rows, True)

    fetch(queries, q_in, blocks_ref, rows, jnp.asarray(HD**-0.5, bf16))
    fetch(keys, k_in, blocks_ref, rows)
    fetch(values, v_in, blocks_ref, rows)
    fetch(context, c_in, blocks_ref, rows)
    fetch(grads, g_in, blocks_ref, rows)
    head_of = lax.broadcasted_iota(jnp.int32, (8, 128), 1) // HD
    chosen = (head_of == lax.broadcasted_iota(jnp.int32, (8, 128), 0)).astype(f32)
    inner = lax.dot_general(
        chosen,
        context[...].astype(f32) * grads[...].astype(f32),
        (((1,), (1,)), ((), ())),
        precision=lax.Precision.HIGHEST,
        preferred_element_type=f32,
    )
    grad_k[...] = jnp.zeros_like(grad_k)
    grad_v[...] = jnp.zeros_like(grad_v)
    for i in range(length // rows):
        here, until = pl.ds(i * rows, rows), pl.ds(0, (i + 1) * rows)
        chances, slants, heads_q, heads_g, heads_k = [], [], [], [], []
        for e in range(2):
            slope = slopes_ref[2 * pair + e]
            query = only_head(queries[here, :], e)
            grad = only_head(grads[here, :], e)
            scores = dot_nt(keys[until, :], query)
            scores = scores - slope * far[until, here] - log_in[0, e : e + 1, here]
            chance = jnp.exp(scores)
            grad_chance = dot_nt(values[until, :], grad)
            slant = chance * (grad_chance - inner[e : e + 1, i * rows : (i + 1) * rows])
            chances.append(chance.astype(bf16))
            slants.append(slant.astype(bf16))
            heads_q.append(query)
            heads_g.append(grad)
            heads_k.append(only_head(keys[until, :], e))
        grad_v[until, :] += dot(jnp.concatenate(chances, axis=1), jnp.concatenate(heads_g, axis=0))
        grad_k[until, :] += dot(jnp.concatenate(slants, axis=1), jnp.concatenate(heads_q, axis=0))
        grad_q[here, :] = (
            dot_tn(slants[0], heads_k[0]) + dot_tn(slants[1], heads_k[1])
        ) * HD**-0.5
    slots = q_in[0].shape[0] // rows
    for b in range(count * slots):
        place = pl.ds(pl.multiple_of(blocks_ref[b] * rows, rows), rows)
        for n, part in enumerate((grad_q, grad_k, grad_v)):
            column = pl.ds(pl.multiple_of(n * width + pair * 128, 128), 128)
            grad_out[b // slots][pl.ds((b % slots) * rows, rows), column] = part[place, :].astype(
                bf16
            )


def attention_specs(joined, segment_ids):
    count, rows_of_piece = len(joined), joined[0].shape[0]
    pairs = joined[0].shape[1] // (3 * 128)
    length = segment_ids.shape[0]
    smem = pl.BlockSpec(memory_space=pltpu.SMEM)
    common = [
        smem,
        smem,
        pl.BlockSpec((length, 1), lambda p: (0, 0)),
        pl.BlockSpec((1, length), lambda p: (0, 0)),
    ]

    def column(n):
        return pl.BlockSpec((rows_of_piece, 128), lambda p: (0, n * pairs + p))

    log_spec = pl.BlockSpec((1, 8, length), lambda p: (p, 0, 0))
    return count, rows_of_piece, pairs, length, common, column, log_spec


def attend(joined, order, segment_ids, slopes):
    count, piece, pairs, length, common, column, log_spec = attention_specs(joined, segment_ids)
    rows = length // order.shape[0]
    low = pltpu.VMEM((length, 128), bf16)
    out = pl.pallas_call(
        partial(attend_kernel, count, rows),
        grid=(pairs,),
        in_specs=common + [column(n) for n in range(3) for _ in range(count)],
        out_specs=[column(0)] * count + [log_spec],
        out_shape=[jax.ShapeDtypeStruct((piece, pairs * 128), bf16)] * count
        + [jax.ShapeDtypeStruct((pairs, 8, length), f32)],
        scratch_shapes=[low, low, low, low, pltpu.VMEM((length, length), f32)],
        compiler_params=pltpu.CompilerParams(vmem_limit_bytes=18 * MIB),
        cost_estimate=pl.CostEstimate(
            flops=pairs * 128 * length,
            bytes_accessed=length * pairs * 128,
            transcendentals=0,
        ),
        name="attend",
    )(order, slopes, segment_ids[:, None], segment_ids[None], *joined, *joined, *joined)
    return out[:count], out[count]


def attend_back(joined, context, logs, grad_context, order, segment_ids, slopes):
    count, piece, pairs, length, common, column, log_spec = attention_specs(joined, segment_ids)
    rows = length // order.shape[0]
    low, high = pltpu.VMEM((length, 128), bf16), pltpu.VMEM((length, 128), f32)
    whole = pl.BlockSpec((piece, 3 * pairs * 128), lambda p: (0, 0))
    out = pl.pallas_call(
        partial(attend_back_kernel, count, rows),
        grid=(pairs,),
        in_specs=common
        + [column(n) for n in range(3) for _ in range(count)]
        + [column(0)] * (2 * count)
        + [log_spec],
        out_specs=[whole] * count,
        out_shape=[jax.ShapeDtypeStruct((piece, 3 * pairs * 128), bf16)] * count,
        scratch_shapes=[low] * 5 + [pltpu.VMEM((length, length), f32)] + [high] * 3,
        compiler_params=pltpu.CompilerParams(vmem_limit_bytes=18 * MIB),
        cost_estimate=pl.CostEstimate(
            flops=pairs * 128 * length,
            bytes_accessed=length * pairs * 128,
            transcendentals=0,
        ),
        name="attend_back",
    )(
        order,
        slopes,
        segment_ids[:, None],
        segment_ids[None],
        *joined,
        *joined,
        *joined,
        *context,
        *grad_context,
        logs,
    )
    return out


def head_group(normed, group, places, segment_ids):
    joined_w, joined_b, out_w, slopes = group
    joined = [(dot(part, joined_w) + joined_b).astype(bf16) for part in normed]
    context, log_total = attend(joined, places, segment_ids, slopes)
    return joined, context, log_total, out_w


def forward(hidden, weights, normed, parts):
    _, _, gain_two, bias_two, _, _, _, out_b, up_w, up_b, down_w, down_b = weights
    middle = (
        hidden
        + scatter_sum(lambda k: sum(dot(part[1][k], part[3]) for part in parts))
        + out_b
    )
    spread = gather_rows(layer_norm(middle, gain_two, bias_two).astype(bf16))
    active, bent = [], []
    for part in spread:
        act, slope = gelu_pair(dot(part, up_w) + up_b)
        act, slope = lax.optimization_barrier((act.astype(bf16), slope.astype(bf16)))
        active.append(act)
        bent.append(slope)
    result = middle + scatter_sum(lambda k: dot(active[k], down_w)) + down_b
    kept = (hidden, normed, *parts[0][:3], middle, spread, active, bent)
    return result, kept


def backward(grad, kept, weights, places, segment_ids, slopes, sums=None, wholes=None):
    hidden, normed, joined, context, log_total, middle, spread, active, bent = kept
    gain_one, bias_one, gain_two, bias_two, joined_w, joined_b, out_w, out_b = weights[:8]
    up_w, up_b, down_w, down_b = weights[8:]
    count = len(normed)

    grad_down_b = jnp.sum(grad, axis=0)
    grads = gather_rows(grad.astype(bf16))
    rows, units, width = out_w.shape[0] // 2, down_w.shape[0] // 2, out_w.shape[1]
    tasks = sums.tasks if sums else []
    whole_normed, whole_context, whole_spread, whole_active = wholes or [None] * 4
    whole_grads = jnp.concatenate(grads)
    for c in range(0, units, 2 * rows):
        tasks.append(
            lambda at, fence, c=c: dot(
                whole_active[at * units + c : at * units + c + 2 * rows], fence(whole_grads)
            )
        )
    if sums:
        sums.par()
        sums.swap()
        sums.own()
        sums.par()
    grad_pre = [
        lax.optimization_barrier(
            (dot_nt(grads[k], down_w) * bent[k].astype(f32)).astype(bf16)
        )
        for k in range(count)
    ]
    up_b_grad = sum(jnp.sum(part, axis=0, dtype=f32) for part in grad_pre)
    whole_pre = jnp.concatenate(grad_pre)
    high = 2 * rows * width // units
    for c in range(0, width, high):
        tasks.append(
            lambda at, fence, c=c: dot(
                fence(whole_spread)[c : c + high], whole_pre[:, at * units : (at + 1) * units]
            ).reshape(2 * rows, width)
        )
    grad_spread = scatter_sum(lambda k: dot_nt(grad_pre[k], up_w))
    grad_two, gain_two_grad, bias_two_grad = layer_norm_back(middle, gain_two, grad_spread)
    grad_middle = grad + grad_two
    out_b_grad = jnp.sum(grad_middle, axis=0)
    grads = gather_rows(grad_middle.astype(bf16))
    if sums:
        sums.own()
        sums.par()
        sums.par()
        sums.step(prepare=False)
        grads[0] = after(grads[0], sums.sent[0], sums.owns[1], sums.pars[3])
    grad_context = [dot_nt(part, out_w).astype(bf16) for part in grads]
    grad_joined = attend_back(
        joined, context, log_total, grad_context, places, segment_ids, slopes
    )
    whole_middle, whole_joined = jnp.concatenate(grads), jnp.concatenate(grad_joined)

    def of_joined(n, at, fence):
        first = (2 * n + at) * rows
        return dot_tn(whole_joined[:, first : first + rows], fence(whole_normed)).astype(bf16)

    def of_out(at, fence):
        left = whole_context[at * rows : (at + 1) * rows]
        return dot(left, fence(whole_middle)).astype(bf16)

    tasks.append(
        lambda at, fence: jnp.concatenate([of_out(at, fence), of_joined(0, at, fence)])
    )
    last_parts = lambda at, fence: [of_joined(1, at, fence), of_joined(2, at, fence)]
    if sums:
        made = sums.step(grad_joined[0]) + sums.from_centre[:1]
        grad_joined = [after(part, *made) for part in grad_joined]
    joined_b_grad = sum(jnp.sum(part, axis=0, dtype=f32) for part in grad_joined)
    grad_normed = scatter_sum(lambda k: dot_nt(grad_joined[k], joined_w))
    if sums:
        sums.step()
    grad_one, gain_one_grad, bias_one_grad = layer_norm_back(hidden, gain_one, grad_normed)
    halves = (joined_b_grad, up_b_grad)
    shared = (
        gain_one_grad,
        bias_one_grad,
        gain_two_grad,
        bias_two_grad,
        out_b_grad,
        grad_down_b,
    )
    return grad_middle + grad_one, last_parts, halves, shared


def local(
    boundary,
    segments,
    gains,
    biases,
    qkv_weight,
    qv_bias,
    out_weight,
    out_bias,
    up_weight,
    up_bias,
    down_weight,
    down_bias,
):
    first = lax.axis_index("section") == 0
    tensor = lax.axis_size("tensor")
    ranks = tensor // 2
    place = lax.axis_index("tensor")
    half, rank = place // ranks, place % ranks
    micro_count, own_rows, width = boundary.shape[1], boundary.shape[3], boundary.shape[4]
    heads = qkv_weight.shape[2] // (3 * HD)
    hidden_units = up_weight.shape[2]

    rows = boundary[0, :, 0]
    mine = jnp.where(half == 0, rows[0], rows[1])
    other = jnp.where(half == 0, rows[1], rows[0])

    order = [(rank + k) % ranks for k in range(ranks)]
    blocks = [b for r in order for b in (half * ranks + r, (1 - half) * ranks + r)]
    places = jnp.stack(blocks)
    segment_ids = jnp.where(half == 0, segments[0, 0], segments[1, 0])
    partner = (1 - half) * ranks + rank
    head_index = jnp.concatenate(
        [p * heads + lax.iota(jnp.int32, heads) for p in (place, partner)]
    )
    slopes = jnp.exp2(-8.0 * (head_index + 1).astype(f32) / H)

    def share(array, row=0):
        part = (array.shape[1] - row) // lax.axis_size("dp")
        at = row + lax.axis_index("dp") * part
        return lax.dynamic_slice(array, (0, at, 0), (1, part, array.shape[2]))[0]

    def arrange(joined):
        return joined.reshape(-1, heads, 3, HD).transpose(0, 2, 1, 3).reshape(joined.shape)

    up_rows, down_rows = width // 2, hidden_units // 2
    own_share = arrange(share(qkv_weight))
    joined_share = swap_half(own_share)
    thin = jnp.concatenate([qv_bias[0].reshape(-1), up_bias[0]])
    pair = qv_bias.shape[2]
    pieces, rest = [], thin
    for _ in range(3):
        pieces.append(lax.reduce_precision(rest, 8, 7))
        rest = rest - pieces[-1]
    pieces = jnp.concatenate(pieces).astype(bf16)
    thin_lines = -(-pieces.size // (16 * width)) * 16
    pieces = jnp.pad(pieces, (0, thin_lines * width - pieces.size)).reshape(thin_lines, width)
    mixed = swap_half(after(jnp.concatenate([other, out_weight[0], pieces]), own_share))
    other_end, other_out = mixed[:own_rows], mixed[own_rows:-thin_lines]
    pieces = mixed[-thin_lines:].reshape(-1)[: 3 * thin.size].reshape(3, -1).astype(f32)
    thin_other = pieces[0] + pieces[1] + pieces[2]
    up_piece, down_piece = share(up_weight, up_rows), share(down_weight, down_rows)
    up_lines = up_piece.size // width
    mixed_share = swap_half(
        after(jnp.concatenate([up_piece.reshape(-1, width), down_piece]), own_share)
    )
    up_direct = up_weight[0, :up_rows].reshape(-1, width)
    direct = swap_half(
        after(jnp.concatenate([up_direct, down_weight[0, :down_rows]]), joined_share)
    )
    other_up = direct[: up_direct.shape[0]].reshape(up_rows, hidden_units)
    other_down = direct[up_direct.shape[0] :]
    own_joined = arrange(qkv_weight[0])

    def passed_round(shares, whole, row, column):
        for step, part in enumerate(shares):
            at = (lax.axis_index("dp") - step) % len(shares)
            whole = lax.dynamic_update_slice(whole, part, (row + at * part.shape[0], column))
        return whole

    none = jnp.zeros((), bf16)
    joined_shares = from_all(joined_share, "dp")
    mixed_shares = from_all(after(mixed_share, *joined_shares[1:]), "dp")
    other_joined = passed_round(joined_shares, jnp.zeros_like(own_joined), 0, 0)
    other_joined = lax.optimization_barrier(other_joined)
    own_end = jnp.concatenate([mine, after(other_end, joined_share)]).astype(f32)
    nothing = jnp.zeros((pair,), f32)
    own_b = jnp.concatenate([thin[:pair], nothing, thin[pair : 2 * pair]])
    other_b = jnp.concatenate([thin_other[:pair], nothing, thin_other[pair : 2 * pair]])
    joined_b = jnp.concatenate([own_b.reshape(3, -1), other_b.reshape(3, -1)], axis=1).reshape(-1)
    up_b = jnp.concatenate([thin[2 * pair :], thin_other[2 * pair :]])
    weights = (gains[0, 1], biases[0, 1], gains[0, 2], biases[0, 2])

    spread_total = variance_total(after(rows, joined_share).astype(f32))
    spread_total = jnp.where(first, spread_total, 0.0)
    token_count = micro_count * own_rows * tensor * lax.axis_size("dp")
    stat = butterfly(jnp.broadcast_to(spread_total, (1, 128)), "section")
    own_b = after(own_b, stat)
    start = layer_norm(own_end, gains[0, 0], biases[0, 0])
    normed = gather_rows(layer_norm(start, weights[0], weights[1]).astype(bf16))
    own_group = (own_joined, own_b, out_weight[0], slopes[:heads])
    own_part = head_group(normed, own_group, places, segment_ids)
    other_b = after(other_b, own_part[1][0])
    other_group = (other_joined, other_b, other_out, slopes[heads:])
    other_part = head_group(normed, other_group, places, segment_ids)

    up_shares = [part[:up_lines].reshape(-1, hidden_units) for part in mixed_shares]
    down_shares = [part[up_lines:] for part in mixed_shares]
    up_w = jnp.pad(other_up, ((0, width - up_rows), (0, 0)))
    up_w = jnp.concatenate([up_weight[0], passed_round(up_shares, up_w, up_rows, 0)], axis=1)
    down_w = jnp.concatenate([down_weight[0], other_down])
    down_w = jnp.pad(down_w, ((0, hidden_units - down_rows), (0, 0)))
    down_w = passed_round(down_shares, down_w, hidden_units + down_rows, 0)
    joined_w = jnp.concatenate(
        [own_joined.reshape(width, 3, -1), other_joined.reshape(width, 3, -1)], axis=2
    ).reshape(width, -1)
    out_w = jnp.concatenate([out_weight[0], other_out], axis=0)
    joined_w, out_w, up_w, down_w = [
        lax.optimization_barrier(part) for part in (joined_w, out_w, up_w, down_w)
    ]
    weights += (joined_w, joined_b, out_w, out_bias[0], up_w, up_b, down_w, down_bias[0])
    result, _ = forward(start, weights, normed, (own_part, other_part))
    stat = after(stat, result)
    for axis in ("tensor", "dp"):
        stat = butterfly(stat, axis)
    embed_stat = stat[0, 0] / token_count
    passed = after(from_section(result.astype(bf16), 1), stat, joined_w, out_w).astype(f32)
    hidden = jnp.where(first, start, passed)
    normed = gather_rows(layer_norm(hidden, weights[0], weights[1]).astype(bf16))
    whole_part = head_group(normed, (joined_w, joined_b, out_w, slopes), places, segment_ids)
    result, kept = forward(hidden, weights, normed, (whole_part,))
    final = layer_norm(result, gains[0, 0], biases[0, 0])

    grad_last, gain_last, bias_last = layer_norm_back(result, gains[0, 0], own_end)
    grad_passed = backward(grad_last, kept, weights, places, segment_ids, slopes)[0]
    normed, context, spread, active = kept[1], kept[3], kept[6], kept[7]
    wholes = [jnp.concatenate(normed)] + [
        jnp.concatenate([part.T for part in parts], axis=1) for parts in (context, spread, active)
    ]
    arrived = after(from_section(grad_passed.astype(bf16), -1), *wholes).astype(f32)
    grad = jnp.where(first, arrived, grad_last)
    sums = RowSums("dp")
    grad_start, last_parts, halves, shared = backward(
        grad, kept, weights, places, segment_ids, slopes, sums, wholes
    )
    grad_entry, gain_first, bias_first = layer_norm_back(own_end, gains[0, 0], grad_start)

    ends = jnp.where(first, grad_entry, final)
    ends_mine = ends[:own_rows]
    ends_other = ends[own_rows:].astype(bf16)
    joined_b_grad, up_b_grad = halves
    joined_b_grad = joined_b_grad.reshape(3, 2, pair)
    up_b_grad = up_b_grad.reshape(2, hidden_units)
    shared = jnp.stack(
        [jnp.where(first, gain_first, gain_last), jnp.where(first, bias_first, bias_last), *shared]
    )
    shared = butterfly(shared, "tensor", 2).reshape(-1)
    thin_size = 2 * pair + hidden_units
    thin_rows = -(-(8 * width + thin_size) // (16 * width)) * 16

    def last_task(at, fence):
        line = [shared, joined_b_grad[0, at], joined_b_grad[2, at], up_b_grad[at]]
        line.append(jnp.zeros((thin_rows * width - 8 * width - thin_size,), f32))
        line = jnp.concatenate(line).astype(bf16)
        return jnp.concatenate(last_parts(at, fence) + [line.reshape(thin_rows, width)])

    sums.tasks.append(last_task)
    sums.step()
    sums.step(ends, shared, joined_b_grad)
    while len(sums.swapped) < len(sums.tasks):
        sums.step()
    ends_other = swap_half(after(ends_other, sums.sent[-1])).astype(f32)
    ends_out = jnp.stack(
        [
            jnp.where(half == 0, ends_mine, ends_other),
            jnp.where(half == 0, ends_other, ends_mine),
        ]
    )[None, :, None]
    summed = [part.astype(f32) for part in sums.finish()]
    thin_grad = summed[-1][-thin_rows:].reshape(-1)
    shared = thin_grad[: 8 * width].reshape(8, width)
    thin_grad = thin_grad[8 * width : 8 * width + thin_size]
    middle_at = len(summed) // 2 - 1
    down_grad = jnp.concatenate(summed[:middle_at])
    up_grad = jnp.concatenate(
        [part.reshape(-1, hidden_units) for part in summed[middle_at:-2]]
    )
    rest = jnp.concatenate([summed[-2], summed[-1][:-thin_rows]]).reshape(4, heads * HD, width)
    out_grad = rest[0]
    joined_grad = rest[1:].reshape(3, heads, HD, width).transpose(3, 1, 0, 2).reshape(width, -1)

    gain_grads = jnp.stack([shared[0], shared[2], shared[4]])[None]
    bias_grads = jnp.stack([shared[1], shared[3], shared[5]])[None]
    return (
        ends_out,
        embed_stat,
        gain_grads,
        bias_grads,
        joined_grad[None],
        thin_grad[: 2 * pair].reshape(1, 2, pair),
        out_grad[None],
        shared[6][None],
        up_grad[None],
        thin_grad[2 * pair :][None],
        down_grad[None],
        shared[7][None],
    )


def solution(mesh):
    return jax.shard_map(
        local,
        mesh=mesh,
        in_specs=(
            P("section", None, "dp", "tensor", None),
            P(None, "dp", None),
            P("section", None, None),
            P("section", None, None),
            P("section", None, "tensor"),
            P("section", None, "tensor"),
            P("section", "tensor", None),
            P("section", None),
            P("section", None, "tensor"),
            P("section", "tensor"),
            P("section", "tensor", None),
            P("section", None),
        ),
        out_specs=(
            P("section", None, "dp", "tensor", None),
            P(),
            P("section", None, None),
            P("section", None, None),
            P("section", None, "tensor"),
            P("section", None, "tensor"),
            P("section", "tensor", None),
            P("section", None),
            P("section", None, "tensor"),
            P("section", "tensor"),
            P("section", "tensor", None),
            P("section", None),
        ),
        check_vma=False,
    )
```

```python
from functools import partial

import jax
import jax.numpy as jnp
from jax import lax
from jax.experimental import pallas as pl
from jax.experimental.pallas import tpu as pltpu
from jax.sharding import PartitionSpec as P

H = 16
HD = 64
eps = 1e-05

f32 = jnp.float32
bf16 = jnp.bfloat16

MIB = 1024 * 1024


def swap_half(array):
    size = lax.axis_size("tensor")
    pairs = [(i, (i + size // 2) % size) for i in range(size)]
    return lax.ppermute(array, "tensor", pairs)


def from_rank(array, by):
    size = lax.axis_size("tensor")
    ranks = size // 2
    pairs = [
        (m * ranks + (j + by) % ranks, m * ranks + j) for m in range(2) for j in range(ranks)
    ]
    return lax.ppermute(array, "tensor", pairs)


def from_section(array, by):
    size = lax.axis_size("section")
    pairs = [(i, i + by) for i in range(size) if 0 <= i + by < size]
    return lax.ppermute(array, "section", pairs)


def gather_rows(own):
    ranks = lax.axis_size("tensor") // 2
    return [own] + [from_rank(own, k) for k in range(1, ranks)]


def scatter_sum(part_of):
    ranks = lax.axis_size("tensor") // 2
    arrived = [from_rank(part_of(k).astype(bf16), ranks - k) for k in range(1, ranks)]
    own = lax.optimization_barrier(part_of(0))
    return own + sum(part.astype(f32) for part in arrived)


def butterfly(array, axis, parts=1):
    size = lax.axis_size(axis)
    step = 1
    while step < size // parts:
        array = array + lax.ppermute(array, axis, [(i, i ^ step) for i in range(size)])
        step *= 2
    return array


def from_all(share, axis):
    size = lax.axis_size(axis)
    shares = [share]
    for by in range(1, size):
        shares.append(lax.ppermute(share, axis, [(i, (i + by) % size) for i in range(size)]))
    return shares


def after(array, *others):
    return lax.optimization_barrier((array, *others))[0]


def total(*parts):
    return sum(part.astype(f32) for part in parts)


class RowSums:
    ends = [(0, 1), (1, 0), (2, 3), (3, 2)]
    centre = [(1, 2), (2, 1)]

    def __init__(self, axis):
        self.axis = axis
        self.line = lax.axis_size(axis) == 4
        place = lax.axis_index(axis)
        self.outer = (place == 0) | (place == 3)
        self.tasks, self.owns, self.pars = [], [], []
        self.swapped, self.partials, self.sent = [], [], []
        self.from_end, self.from_centre = [], []

    def part(self, done, at, others):
        if len(done) < len(self.tasks):
            fence = (lambda array: after(array, *others)) if others else lambda array: array
            part = self.tasks[len(done)](at, fence).astype(bf16)
            done.append(lax.optimization_barrier(part))

    def own(self, *others):
        self.part(self.owns, 0, others)

    def par(self, *others):
        self.part(self.pars, 1, others)

    def swap(self, *others):
        part = self.pars[len(self.swapped)]
        self.swapped.append(swap_half(after(part, *others) if others else part))

    def step(self, *others, prepare=True):
        step, count = len(self.sent), len(self.tasks)
        come = self.swapped[step : step + 1] + self.from_end[-1:] + self.from_centre[-1:]
        come += list(others)
        fresh = total(self.owns[step], self.swapped[step]) if step < count else None
        if not self.line:
            self.sent.append(fresh.astype(bf16))
            come = self.swapped[step : step + 1]
        else:
            done = total(self.partials[step - 2], self.from_centre[step - 2]) if step >= 2 else fresh
            if fresh is None:
                fresh = done
            done = jnp.pad(done, ((0, fresh.shape[0] - done.shape[0]), (0, 0)))
            to_end = jnp.where(self.outer, fresh, done).astype(bf16)
            self.sent.append(after(to_end, *come))
            self.from_end.append(lax.ppermute(self.sent[-1], self.axis, self.ends))
            if 0 <= step - 1 < count:
                parts = (self.owns[step - 1], self.swapped[step - 1], self.from_end[step - 1])
                self.partials.append(total(*parts).astype(bf16))
                middle = after(self.partials[-1], *come)
                self.from_centre.append(lax.ppermute(middle, self.axis, self.centre))
        while len(self.swapped) < min(step + 3, len(self.pars)):
            self.swap(*come)
        made = self.sent[-1:] + self.partials[-1:]
        if prepare:
            self.own(*made)
            self.par(*made)
        return made

    def finish(self):
        count = len(self.tasks)
        while len(self.sent) < count + (2 if self.line else 0):
            self.step()
        if not self.line:
            return [lax.psum(chunk, self.axis) for chunk in self.sent]
        sums = [
            jnp.where(self.outer, self.from_end[n + 2], self.sent[n + 2]) for n in range(count)
        ]
        return [part[: self.owns[n].shape[0]] for n, part in enumerate(sums)]


def dot(left, right):
    return jnp.dot(left, right, preferred_element_type=f32)


def dot_nt(left, right):
    return lax.dot_general(left, right, (((1,), (1,)), ((), ())), preferred_element_type=f32)


def dot_tn(left, right):
    return lax.dot_general(left, right, (((0,), (0,)), ((), ())), preferred_element_type=f32)


def normalise(values_in):
    centre = jnp.mean(values_in, axis=-1, keepdims=True)
    centred = values_in - centre
    variance = jnp.mean(centred * centred, axis=-1, keepdims=True)
    scale = lax.rsqrt(variance + eps)
    return centred * scale, scale


def layer_norm(values_in, gain, bias):
    return normalise(values_in)[0] * gain + bias


def layer_norm_back(values_in, gain, grad):
    hat, scale = normalise(values_in)
    scaled = grad * gain
    inner = jnp.mean(scaled, axis=-1, keepdims=True)
    along = jnp.mean(scaled * hat, axis=-1, keepdims=True)
    grad_in = scale * (scaled - inner - hat * along)
    return grad_in, jnp.sum(grad * hat, axis=0), jnp.sum(grad, axis=0)


def variance_total(values_in):
    centred = values_in - jnp.mean(values_in, axis=-1, keepdims=True)
    return jnp.sum(jnp.mean(centred * centred, axis=-1))


def gelu_pair(pre):
    root = 0.7978845608028654
    square = pre * pre
    bent = jnp.tanh(pre * (root + root * 0.044715 * square))
    rise = 0.5 + 0.5 * bent
    slope = rise * (1.0 + pre * (1.0 - bent) * (root + 3 * root * 0.044715 * square))
    return pre * rise, slope


def fetch(scratch, pieces, blocks_ref, rows, scale=None):
    slots = pieces[0].shape[0] // rows
    for b in range(len(pieces) * slots):
        part = pieces[b // slots][pl.ds((b % slots) * rows, rows), :]
        if scale is not None:
            part = part * scale
        scratch[pl.ds(pl.multiple_of(blocks_ref[b] * rows, rows), rows), :] = part


def only_head(values, e):
    lane = lax.broadcasted_iota(jnp.int32, values.shape, 1)
    return jnp.where((lane >= HD) == (e == 1), values, jnp.zeros_like(values))


def fill_distance(far, seg_col_ref, seg_row_ref, rows, flipped, span=1):
    length = far.shape[0]
    for one in range(length // rows):
        for two in range(one // span * span + span):
            low, high = pl.ds(one * rows, rows), pl.ds(two * rows, rows)
            if flipped:
                low, high = high, low
            shape = (rows, rows)
            along = lax.broadcasted_iota(jnp.int32, shape, 0) - lax.broadcasted_iota(
                jnp.int32, shape, 1
            )
            gap = (-along if flipped else along) + (one - two) * rows
            same = seg_col_ref[low, :] == seg_row_ref[:, high]
            far[low, high] = jnp.where(same & (gap >= 0), gap.astype(f32), 1e32)


def attend_kernel(count, rows, blocks_ref, slopes_ref, seg_col_ref, seg_row_ref, *refs):
    q_in, k_in, v_in = refs[:count], refs[count : 2 * count], refs[2 * count : 3 * count]
    context_out = refs[3 * count : 4 * count]
    log_out = refs[4 * count]
    queries, keys, values, context, far = refs[4 * count + 1 :]
    pair = pl.program_id(0)
    length = queries.shape[0]

    @pl.when(pair == 0)
    def _():
        fill_distance(far, seg_col_ref, seg_row_ref, rows, False, 2)

    fetch(queries, q_in, blocks_ref, rows, jnp.asarray(HD**-0.5, bf16))
    fetch(keys, k_in, blocks_ref, rows)
    fetch(values, v_in, blocks_ref, rows)
    many = 2 * rows
    lane = lax.broadcasted_iota(jnp.int32, (many, 128), 1)
    for i in range(length // many):
        here, until = pl.ds(i * many, many), pl.ds(0, (i + 1) * many)
        total = None
        logs = None
        for e in range(2):
            slope = slopes_ref[2 * pair + e]
            scores = dot_nt(only_head(queries[here, :], e), keys[until, :])
            scores = scores - slope * far[here, until]
            highest = jnp.max(scores, axis=1, keepdims=True)
            shifted = jnp.exp(scores - highest)
            summed = jnp.sum(shifted, axis=1, keepdims=True)
            part = dot(shifted.astype(bf16), only_head(values[until, :], e)) / summed
            log = highest + jnp.log(summed)
            total = part if e == 0 else total + part
            logs = jnp.broadcast_to(log, (many, 128)) if e == 0 else jnp.where(lane == 1, log, logs)
        context[here, :] = total.astype(bf16)
        log_out[0, :, here] = logs.T[:8]
    slots = q_in[0].shape[0] // rows
    for b in range(count * slots):
        context_out[b // slots][pl.ds((b % slots) * rows, rows), :] = context[
            pl.ds(pl.multiple_of(blocks_ref[b] * rows, rows), rows), :
        ]


def attend_back_kernel(count, rows, blocks_ref, slopes_ref, seg_col_ref, seg_row_ref, *refs):
    q_in, k_in, v_in, c_in, g_in = [refs[n * count : (n + 1) * count] for n in range(5)]
    log_in = refs[5 * count]
    grad_out = refs[5 * count + 1 : 6 * count + 1]
    queries, keys, values, context, grads, far, grad_q, grad_k, grad_v = refs[6 * count + 1 :]
    pair = pl.program_id(0)
    length = queries.shape[0]
    width = grad_out[0].shape[1] // 3

    @pl.when(pair == 0)
    def _():
        fill_distance(far, seg_col_ref, seg_row_ref, rows, True)

    fetch(queries, q_in, blocks_ref, rows, jnp.asarray(HD**-0.5, bf16))
    fetch(keys, k_in, blocks_ref, rows)
    fetch(values, v_in, blocks_ref, rows)
    fetch(context, c_in, blocks_ref, rows)
    fetch(grads, g_in, blocks_ref, rows)
    head_of = lax.broadcasted_iota(jnp.int32, (8, 128), 1) // HD
    chosen = (head_of == lax.broadcasted_iota(jnp.int32, (8, 128), 0)).astype(f32)
    inner = lax.dot_general(
        chosen,
        context[...].astype(f32) * grads[...].astype(f32),
        (((1,), (1,)), ((), ())),
        precision=lax.Precision.HIGHEST,
        preferred_element_type=f32,
    )
    grad_k[...] = jnp.zeros_like(grad_k)
    grad_v[...] = jnp.zeros_like(grad_v)
    for i in range(length // rows):
        here, until = pl.ds(i * rows, rows), pl.ds(0, (i + 1) * rows)
        chances, slants, heads_q, heads_g, heads_k = [], [], [], [], []
        for e in range(2):
            slope = slopes_ref[2 * pair + e]
            query = only_head(queries[here, :], e)
            grad = only_head(grads[here, :], e)
            scores = dot_nt(keys[until, :], query)
            scores = scores - slope * far[until, here] - log_in[0, e : e + 1, here]
            chance = jnp.exp(scores)
            grad_chance = dot_nt(values[until, :], grad)
            slant = chance * (grad_chance - inner[e : e + 1, i * rows : (i + 1) * rows])
            chances.append(chance.astype(bf16))
            slants.append(slant.astype(bf16))
            heads_q.append(query)
            heads_g.append(grad)
            heads_k.append(only_head(keys[until, :], e))
        grad_v[until, :] += dot(jnp.concatenate(chances, axis=1), jnp.concatenate(heads_g, axis=0))
        grad_k[until, :] += dot(jnp.concatenate(slants, axis=1), jnp.concatenate(heads_q, axis=0))
        grad_q[here, :] = (
            dot_tn(slants[0], heads_k[0]) + dot_tn(slants[1], heads_k[1])
        ) * HD**-0.5
    slots = q_in[0].shape[0] // rows
    for b in range(count * slots):
        place = pl.ds(pl.multiple_of(blocks_ref[b] * rows, rows), rows)
        for n, part in enumerate((grad_q, grad_k, grad_v)):
            column = pl.ds(pl.multiple_of(n * width + pair * 128, 128), 128)
            grad_out[b // slots][pl.ds((b % slots) * rows, rows), column] = part[place, :].astype(
                bf16
            )


def attention_specs(joined, segment_ids):
    count, rows_of_piece = len(joined), joined[0].shape[0]
    pairs = joined[0].shape[1] // (3 * 128)
    length = segment_ids.shape[0]
    smem = pl.BlockSpec(memory_space=pltpu.SMEM)
    common = [
        smem,
        smem,
        pl.BlockSpec((length, 1), lambda p: (0, 0)),
        pl.BlockSpec((1, length), lambda p: (0, 0)),
    ]

    def column(n):
        return pl.BlockSpec((rows_of_piece, 128), lambda p: (0, n * pairs + p))

    log_spec = pl.BlockSpec((1, 8, length), lambda p: (p, 0, 0))
    return count, rows_of_piece, pairs, length, common, column, log_spec


def attend(joined, order, segment_ids, slopes):
    count, piece, pairs, length, common, column, log_spec = attention_specs(joined, segment_ids)
    rows = length // order.shape[0]
    low = pltpu.VMEM((length, 128), bf16)
    out = pl.pallas_call(
        partial(attend_kernel, count, rows),
        grid=(pairs,),
        in_specs=common + [column(n) for n in range(3) for _ in range(count)],
        out_specs=[column(0)] * count + [log_spec],
        out_shape=[jax.ShapeDtypeStruct((piece, pairs * 128), bf16)] * count
        + [jax.ShapeDtypeStruct((pairs, 8, length), f32)],
        scratch_shapes=[low, low, low, low, pltpu.VMEM((length, length), f32)],
        compiler_params=pltpu.CompilerParams(vmem_limit_bytes=18 * MIB),
        cost_estimate=pl.CostEstimate(
            flops=pairs * 128 * length,
            bytes_accessed=length * pairs * 128,
            transcendentals=0,
        ),
        name="attend",
    )(order, slopes, segment_ids[:, None], segment_ids[None], *joined, *joined, *joined)
    return out[:count], out[count]


def attend_back(joined, context, logs, grad_context, order, segment_ids, slopes):
    count, piece, pairs, length, common, column, log_spec = attention_specs(joined, segment_ids)
    rows = length // order.shape[0]
    low, high = pltpu.VMEM((length, 128), bf16), pltpu.VMEM((length, 128), f32)
    whole = pl.BlockSpec((piece, 3 * pairs * 128), lambda p: (0, 0))
    out = pl.pallas_call(
        partial(attend_back_kernel, count, rows),
        grid=(pairs,),
        in_specs=common
        + [column(n) for n in range(3) for _ in range(count)]
        + [column(0)] * (2 * count)
        + [log_spec],
        out_specs=[whole] * count,
        out_shape=[jax.ShapeDtypeStruct((piece, 3 * pairs * 128), bf16)] * count,
        scratch_shapes=[low] * 5 + [pltpu.VMEM((length, length), f32)] + [high] * 3,
        compiler_params=pltpu.CompilerParams(vmem_limit_bytes=18 * MIB),
        cost_estimate=pl.CostEstimate(
            flops=pairs * 128 * length,
            bytes_accessed=length * pairs * 128,
            transcendentals=0,
        ),
        name="attend_back",
    )(
        order,
        slopes,
        segment_ids[:, None],
        segment_ids[None],
        *joined,
        *joined,
        *joined,
        *context,
        *grad_context,
        logs,
    )
    return out


def head_group(normed, group, places, segment_ids):
    joined_w, joined_b, out_w, slopes = group
    joined = [(dot(part, joined_w) + joined_b).astype(bf16) for part in normed]
    context, log_total = attend(joined, places, segment_ids, slopes)
    return joined, context, log_total, out_w


def forward(hidden, weights, normed, parts):
    _, _, gain_two, bias_two, _, _, _, out_b, up_w, up_b, down_w, down_b = weights
    middle = (
        hidden
        + scatter_sum(lambda k: sum(dot(part[1][k], part[3]) for part in parts))
        + out_b
    )
    spread = gather_rows(layer_norm(middle, gain_two, bias_two).astype(bf16))
    active, bent = [], []
    for part in spread:
        act, slope = gelu_pair(dot(part, up_w) + up_b)
        act, slope = lax.optimization_barrier((act.astype(bf16), slope.astype(bf16)))
        active.append(act)
        bent.append(slope)
    result = middle + scatter_sum(lambda k: dot(active[k], down_w)) + down_b
    kept = (hidden, normed, *parts[0][:3], middle, spread, active, bent)
    return result, kept


def backward(grad, kept, weights, places, segment_ids, slopes, sums=None, wholes=None):
    hidden, normed, joined, context, log_total, middle, spread, active, bent = kept
    gain_one, bias_one, gain_two, bias_two, joined_w, joined_b, out_w, out_b = weights[:8]
    up_w, up_b, down_w, down_b = weights[8:]
    count = len(normed)

    grad_down_b = jnp.sum(grad, axis=0)
    grads = gather_rows(grad.astype(bf16))
    rows, units, width = out_w.shape[0] // 2, down_w.shape[0] // 2, out_w.shape[1]
    tasks = sums.tasks if sums else []
    whole_normed, whole_context, whole_spread, whole_active = wholes or [None] * 4
    whole_grads = jnp.concatenate(grads)
    for c in range(0, units, 2 * rows):
        tasks.append(
            lambda at, fence, c=c: dot(
                whole_active[at * units + c : at * units + c + 2 * rows], fence(whole_grads)
            )
        )
    if sums:
        sums.par()
        sums.swap()
        sums.own()
        sums.par()
    grad_pre = [
        lax.optimization_barrier(
            (dot_nt(grads[k], down_w) * bent[k].astype(f32)).astype(bf16)
        )
        for k in range(count)
    ]
    up_b_grad = sum(jnp.sum(part, axis=0, dtype=f32) for part in grad_pre)
    whole_pre = jnp.concatenate(grad_pre)
    high = 2 * rows * width // units
    for c in range(0, width, high):
        tasks.append(
            lambda at, fence, c=c: dot(
                fence(whole_spread)[c : c + high], whole_pre[:, at * units : (at + 1) * units]
            ).reshape(2 * rows, width)
        )
    grad_spread = scatter_sum(lambda k: dot_nt(grad_pre[k], up_w))
    grad_two, gain_two_grad, bias_two_grad = layer_norm_back(middle, gain_two, grad_spread)
    grad_middle = grad + grad_two
    out_b_grad = jnp.sum(grad_middle, axis=0)
    grads = gather_rows(grad_middle.astype(bf16))
    if sums:
        sums.own()
        sums.par()
        sums.par()
        sums.step(prepare=False)
        grads[0] = after(grads[0], sums.sent[0], sums.owns[1], sums.pars[3])
    grad_context = [dot_nt(part, out_w).astype(bf16) for part in grads]
    grad_joined = attend_back(
        joined, context, log_total, grad_context, places, segment_ids, slopes
    )
    whole_middle, whole_joined = jnp.concatenate(grads), jnp.concatenate(grad_joined)

    def of_joined(n, at, fence):
        first = (2 * n + at) * rows
        return dot_tn(whole_joined[:, first : first + rows], fence(whole_normed)).astype(bf16)

    def of_out(at, fence):
        left = whole_context[at * rows : (at + 1) * rows]
        return dot(left, fence(whole_middle)).astype(bf16)

    tasks.append(
        lambda at, fence: jnp.concatenate([of_out(at, fence), of_joined(0, at, fence)])
    )
    last_parts = lambda at, fence: [of_joined(1, at, fence), of_joined(2, at, fence)]
    if sums:
        made = sums.step(grad_joined[0]) + sums.from_centre[:1]
        grad_joined = [after(part, *made) for part in grad_joined]
    joined_b_grad = sum(jnp.sum(part, axis=0, dtype=f32) for part in grad_joined)
    grad_normed = scatter_sum(lambda k: dot_nt(grad_joined[k], joined_w))
    if sums:
        sums.step()
    grad_one, gain_one_grad, bias_one_grad = layer_norm_back(hidden, gain_one, grad_normed)
    halves = (joined_b_grad, up_b_grad)
    shared = (
        gain_one_grad,
        bias_one_grad,
        gain_two_grad,
        bias_two_grad,
        out_b_grad,
        grad_down_b,
    )
    return grad_middle + grad_one, last_parts, halves, shared


def local(
    boundary,
    segments,
    gains,
    biases,
    qkv_weight,
    qv_bias,
    out_weight,
    out_bias,
    up_weight,
    up_bias,
    down_weight,
    down_bias,
):
    first = lax.axis_index("section") == 0
    tensor = lax.axis_size("tensor")
    ranks = tensor // 2
    place = lax.axis_index("tensor")
    half, rank = place // ranks, place % ranks
    micro_count, own_rows, width = boundary.shape[1], boundary.shape[3], boundary.shape[4]
    heads = qkv_weight.shape[2] // (3 * HD)
    hidden_units = up_weight.shape[2]

    rows = boundary[0, :, 0]
    mine = jnp.where(half == 0, rows[0], rows[1])
    other = jnp.where(half == 0, rows[1], rows[0])

    order = [(rank + k) % ranks for k in range(ranks)]
    blocks = [b for r in order for b in (half * ranks + r, (1 - half) * ranks + r)]
    places = jnp.stack(blocks)
    segment_ids = jnp.where(half == 0, segments[0, 0], segments[1, 0])
    partner = (1 - half) * ranks + rank
    head_index = jnp.concatenate(
        [p * heads + lax.iota(jnp.int32, heads) for p in (place, partner)]
    )
    slopes = jnp.exp2(-8.0 * (head_index + 1).astype(f32) / H)

    def share(array, row=0):
        part = (array.shape[1] - row) // lax.axis_size("dp")
        at = row + lax.axis_index("dp") * part
        return lax.dynamic_slice(array, (0, at, 0), (1, part, array.shape[2]))[0]

    def arrange(joined):
        return joined.reshape(-1, heads, 3, HD).transpose(0, 2, 1, 3).reshape(joined.shape)

    up_rows, down_rows = 7 * width // 16, 7 * hidden_units // 16
    own_share = arrange(share(qkv_weight))
    joined_share = swap_half(own_share)
    thin = jnp.concatenate([qv_bias[0].reshape(-1), up_bias[0]])
    pair = qv_bias.shape[2]
    pieces, rest = [], thin
    for _ in range(3):
        pieces.append(lax.reduce_precision(rest, 8, 7))
        rest = rest - pieces[-1]
    pieces = jnp.concatenate(pieces).astype(bf16)
    thin_lines = -(-pieces.size // (16 * width)) * 16
    pieces = jnp.pad(pieces, (0, thin_lines * width - pieces.size)).reshape(thin_lines, width)
    mixed = swap_half(after(jnp.concatenate([other, out_weight[0], pieces]), own_share))
    other_end, other_out = mixed[:own_rows], mixed[own_rows:-thin_lines]
    pieces = mixed[-thin_lines:].reshape(-1)[: 3 * thin.size].reshape(3, -1).astype(f32)
    thin_other = pieces[0] + pieces[1] + pieces[2]
    up_piece, down_piece = share(up_weight, up_rows), share(down_weight, down_rows)
    up_lines = up_piece.size // width
    mixed_share = swap_half(
        after(jnp.concatenate([up_piece.reshape(-1, width), down_piece]), own_share)
    )
    up_direct = up_weight[0, :up_rows].reshape(-1, width)
    direct = swap_half(
        after(jnp.concatenate([up_direct, down_weight[0, :down_rows]]), joined_share)
    )
    other_up = direct[: up_direct.shape[0]].reshape(up_rows, hidden_units)
    other_down = direct[up_direct.shape[0] :]
    own_joined = arrange(qkv_weight[0])

    def passed_round(shares, whole, row, column):
        for step, part in enumerate(shares):
            at = (lax.axis_index("dp") - step) % len(shares)
            whole = lax.dynamic_update_slice(whole, part, (row + at * part.shape[0], column))
        return whole

    none = jnp.zeros((), bf16)
    joined_shares = from_all(joined_share, "dp")
    mixed_shares = from_all(after(mixed_share, *joined_shares[1:]), "dp")
    other_joined = passed_round(joined_shares, jnp.zeros_like(own_joined), 0, 0)
    other_joined = lax.optimization_barrier(other_joined)
    own_end = jnp.concatenate([mine, after(other_end, joined_share)]).astype(f32)
    nothing = jnp.zeros((pair,), f32)
    own_b = jnp.concatenate([thin[:pair], nothing, thin[pair : 2 * pair]])
    other_b = jnp.concatenate([thin_other[:pair], nothing, thin_other[pair : 2 * pair]])
    joined_b = jnp.concatenate([own_b.reshape(3, -1), other_b.reshape(3, -1)], axis=1).reshape(-1)
    up_b = jnp.concatenate([thin[2 * pair :], thin_other[2 * pair :]])
    weights = (gains[0, 1], biases[0, 1], gains[0, 2], biases[0, 2])

    spread_total = variance_total(after(rows, joined_share).astype(f32))
    spread_total = jnp.where(first, spread_total, 0.0)
    token_count = micro_count * own_rows * tensor * lax.axis_size("dp")
    stat = butterfly(jnp.broadcast_to(spread_total, (1, 128)), "section")
    own_b = after(own_b, stat)
    start = layer_norm(own_end, gains[0, 0], biases[0, 0])
    normed = gather_rows(layer_norm(start, weights[0], weights[1]).astype(bf16))
    own_group = (own_joined, own_b, out_weight[0], slopes[:heads])
    own_part = head_group(normed, own_group, places, segment_ids)
    other_b = after(other_b, own_part[1][0])
    other_group = (other_joined, other_b, other_out, slopes[heads:])
    other_part = head_group(normed, other_group, places, segment_ids)

    up_shares = [part[:up_lines].reshape(-1, hidden_units) for part in mixed_shares]
    down_shares = [part[up_lines:] for part in mixed_shares]
    up_w = jnp.pad(other_up, ((0, width - up_rows), (0, 0)))
    up_w = jnp.concatenate([up_weight[0], passed_round(up_shares, up_w, up_rows, 0)], axis=1)
    down_w = jnp.concatenate([down_weight[0], other_down])
    down_w = jnp.pad(down_w, ((0, hidden_units - down_rows), (0, 0)))
    down_w = passed_round(down_shares, down_w, hidden_units + down_rows, 0)
    joined_w = jnp.concatenate(
        [own_joined.reshape(width, 3, -1), other_joined.reshape(width, 3, -1)], axis=2
    ).reshape(width, -1)
    out_w = jnp.concatenate([out_weight[0], other_out], axis=0)
    joined_w, out_w, up_w, down_w = [
        lax.optimization_barrier(part) for part in (joined_w, out_w, up_w, down_w)
    ]
    weights += (joined_w, joined_b, out_w, out_bias[0], up_w, up_b, down_w, down_bias[0])
    result, _ = forward(start, weights, normed, (own_part, other_part))
    stat = after(stat, result)
    for axis in ("tensor", "dp"):
        stat = butterfly(stat, axis)
    embed_stat = stat[0, 0] / token_count
    passed = after(from_section(result.astype(bf16), 1), stat, joined_w, out_w).astype(f32)
    hidden = jnp.where(first, start, passed)
    normed = gather_rows(layer_norm(hidden, weights[0], weights[1]).astype(bf16))
    whole_part = head_group(normed, (joined_w, joined_b, out_w, slopes), places, segment_ids)
    result, kept = forward(hidden, weights, normed, (whole_part,))
    final = layer_norm(result, gains[0, 0], biases[0, 0])

    grad_last, gain_last, bias_last = layer_norm_back(result, gains[0, 0], own_end)
    grad_passed = backward(grad_last, kept, weights, places, segment_ids, slopes)[0]
    normed, context, spread, active = kept[1], kept[3], kept[6], kept[7]
    wholes = [jnp.concatenate(normed)] + [
        jnp.concatenate([part.T for part in parts], axis=1) for parts in (context, spread, active)
    ]
    arrived = after(from_section(grad_passed.astype(bf16), -1), *wholes).astype(f32)
    grad = jnp.where(first, arrived, grad_last)
    sums = RowSums("dp")
    grad_start, last_parts, halves, shared = backward(
        grad, kept, weights, places, segment_ids, slopes, sums, wholes
    )
    grad_entry, gain_first, bias_first = layer_norm_back(own_end, gains[0, 0], grad_start)

    ends = jnp.where(first, grad_entry, final)
    ends_mine = ends[:own_rows]
    ends_other = ends[own_rows:].astype(bf16)
    joined_b_grad, up_b_grad = halves
    joined_b_grad = joined_b_grad.reshape(3, 2, pair)
    up_b_grad = up_b_grad.reshape(2, hidden_units)
    shared = jnp.stack(
        [jnp.where(first, gain_first, gain_last), jnp.where(first, bias_first, bias_last), *shared]
    )
    shared = butterfly(shared, "tensor", 2).reshape(-1)
    thin_size = 2 * pair + hidden_units
    thin_rows = -(-(8 * width + thin_size) // (16 * width)) * 16

    def last_task(at, fence):
        line = [shared, joined_b_grad[0, at], joined_b_grad[2, at], up_b_grad[at]]
        line.append(jnp.zeros((thin_rows * width - 8 * width - thin_size,), f32))
        line = jnp.concatenate(line).astype(bf16)
        return jnp.concatenate(last_parts(at, fence) + [line.reshape(thin_rows, width)])

    sums.tasks.append(last_task)
    sums.step()
    sums.step(ends, shared, joined_b_grad)
    while len(sums.swapped) < len(sums.tasks):
        sums.step()
    ends_other = swap_half(after(ends_other, sums.sent[-1])).astype(f32)
    ends_out = jnp.stack(
        [
            jnp.where(half == 0, ends_mine, ends_other),
            jnp.where(half == 0, ends_other, ends_mine),
        ]
    )[None, :, None]
    summed = [part.astype(f32) for part in sums.finish()]
    thin_grad = summed[-1][-thin_rows:].reshape(-1)
    shared = thin_grad[: 8 * width].reshape(8, width)
    thin_grad = thin_grad[8 * width : 8 * width + thin_size]
    middle_at = len(summed) // 2 - 1
    down_grad = jnp.concatenate(summed[:middle_at])
    up_grad = jnp.concatenate(
        [part.reshape(-1, hidden_units) for part in summed[middle_at:-2]]
    )
    rest = jnp.concatenate([summed[-2], summed[-1][:-thin_rows]]).reshape(4, heads * HD, width)
    out_grad = rest[0]
    joined_grad = rest[1:].reshape(3, heads, HD, width).transpose(3, 1, 0, 2).reshape(width, -1)

    gain_grads = jnp.stack([shared[0], shared[2], shared[4]])[None]
    bias_grads = jnp.stack([shared[1], shared[3], shared[5]])[None]
    return (
        ends_out,
        embed_stat,
        gain_grads,
        bias_grads,
        joined_grad[None],
        thin_grad[: 2 * pair].reshape(1, 2, pair),
        out_grad[None],
        shared[6][None],
        up_grad[None],
        thin_grad[2 * pair :][None],
        down_grad[None],
        shared[7][None],
    )


def solution(mesh):
    return jax.shard_map(
        local,
        mesh=mesh,
        in_specs=(
            P("section", None, "dp", "tensor", None),
            P(None, "dp", None),
            P("section", None, None),
            P("section", None, None),
            P("section", None, "tensor"),
            P("section", None, "tensor"),
            P("section", "tensor", None),
            P("section", None),
            P("section", None, "tensor"),
            P("section", "tensor"),
            P("section", "tensor", None),
            P("section", None),
        ),
        out_specs=(
            P("section", None, "dp", "tensor", None),
            P(),
            P("section", None, None),
            P("section", None, None),
            P("section", None, "tensor"),
            P("section", None, "tensor"),
            P("section", "tensor", None),
            P("section", None),
            P("section", None, "tensor"),
            P("section", "tensor"),
            P("section", "tensor", None),
            P("section", None),
        ),
        check_vma=False,
    )
```
